256 devices in a mesh: feeder: 16 (over z, core), tm: 16 (over y, x).
Axes of the slice: x: 4, y: 4, z: 8, core: 2. Of those that a mesh axis runs over, the one named last changes fastest.
Arguments:
- node_load: bfloat16 [256, 64, 96, 512], P('feeder', None, 'tm'), may hold values from -6 to 6
- drive_map: bfloat16 [256, 512, 256], P('feeder'), may hold values from -0.25 to 0.25
- decay_rate: float32 [256, 96, 256], P('feeder', 'tm'), may hold values from 0.45 to 1
- counts: int32 [256], P('feeder'), may hold values from 64 to 256
- out_map: float32 [256, 2, 256], P('feeder'), may hold values from -0.375 to 0.375
- area_of: int32 [256, 1], replicated, may hold values from 0 to 15; in each aligned block of 16 rows (0 to 15, 16 to 31, ...) at most 2 rows name the same one
- head_bus: int32 [256], replicated, may hold values from 0 to 255
- rule_of: int32 [256], replicated, may hold values from 0 to 15
- rule_knots: int32 [16, 8], replicated, may hold values from -3200 to 2400, as said below
- levels: int32 [16, 8], replicated, may hold values from -1000 to 1000
- sensitivity: float32 [16, 2, 256, 256], P('feeder'), may hold values from -0.6 to 0.6
Outputs:
- setpoints: float32 [256, 96, 64], P('feeder', 'tm')
The draws below stay inside these ranges and needn't reach their ends.
Inputs may be any that keep to these rules, and one draw needn't show every extreme that they name: `area_of`: in each aligned block of 16 feeders no area is named by more than 2 feeders, a bound that some block reaches. `rule_knots`: each row strictly increasing, neighbouring breakpoints 200 to 800 apart.
All inputs are finite; a program needn't handle non-finite values.
Results may differ from the reference program's by a relative error of at most 0.00045.
Values sent between devices are 32-bit elements; how exact they have to be, the bound alone decides.
No kernel may reach another device: no remote copies, remote signals or barrier semaphores. Data moves between devices by JAX's collectives and lax.ppermute only.
A program may use at most 64 MiB of HBM per device.

```python
import math
import jax
import jax.numpy as jnp
import numpy as np
from jax import lax

NODE = 512
STATE = 256
BUS = 256
CAP = 2
RULES = 16
KNOTS = 8
FEED_DEV = 16
SCEN = 64
LATERAL_COUNT = 256
AREAS = 16
HORIZON_TICKS = 96


def draw_decay_rate(key, part):
    speed_seed, surge_seed, multiplier_seed = jax.random.split(jax.random.fold_in(key, 11), 3)
    lowest = math.log(0.3 / HORIZON_TICKS)
    highest = math.log(1.0 / 30.0)
    spread = jax.random.uniform(speed_seed, (LATERAL_COUNT, 1, STATE), jnp.float32)
    rates = jnp.exp(lowest + (highest - lowest) * spread)
    nominal_magnitude = jnp.exp(-rates)
    surge_size = jax.random.uniform(surge_seed, (LATERAL_COUNT, HORIZON_TICKS, 1), jnp.float32) < 3.0 / HORIZON_TICKS
    multiplier_number = jax.random.uniform(multiplier_seed, (LATERAL_COUNT, HORIZON_TICKS, 1), jnp.float32, 0.5, 0.8)
    return (nominal_magnitude * jnp.where(surge_size, multiplier_number, 1.0)).astype(jnp.float32)


def draw_rule_knots(key, part):
    spacing = jax.random.randint(jax.random.fold_in(key, 23), (RULES, KNOTS), 200, 801).astype(jnp.int32)
    totals = jnp.cumsum(spacing, axis=1).astype(jnp.int32)
    middle = KNOTS // 2
    return (totals - totals[:, middle:middle + 1]).astype(jnp.int32)


def touch_ends(array, rng, smallest, high):
    place = [jax.random.randint(jax.random.fold_in(rng, axis), (), 0, length) for axis, length in enumerate(array.shape)]
    main_axis = array.shape.index(max(array.shape))
    next_to = place[:main_axis] + [(place[main_axis] + 1) % array.shape[main_axis]] + place[main_axis + 1:]
    return array.at[tuple(place)].set(smallest).at[tuple(next_to)].set(high)


def block_levels(rng, dims, cuts, smallest, largest):
    factor_of = 1.0
    for position, parts in cuts:
        heights = jax.random.uniform(jax.random.fold_in(jax.random.fold_in(rng, 6), position), (parts,), jnp.float32, smallest / len(cuts), largest / len(cuts))
        factor_of = factor_of * jnp.repeat(jnp.exp(heights), dims[position] // parts).reshape((-1,) + (1,) * (len(dims) - 1 - position))
    return factor_of


def shared_out(stream_key, own, number, rows, amount, top, bound, skew):
    sequence = jax.random.permutation(stream_key, amount)
    packed, ordinary = shares(amount, rows * top, bound, skew, True), shares(amount, rows * top, bound, skew, False)
    places = jnp.arange(amount)

    def named(lengths, turn):
        used = int((lengths > 0).sum())
        fixed = max(1, used // 4)
        moved = fixed + (places - fixed + turn * (used - fixed)) % max(1, amount - fixed)
        return jnp.zeros((amount,), jnp.int32).at[sequence[jnp.where(places < fixed, places, moved)]].set(jnp.asarray(lengths, jnp.int32))

    lengths = jnp.where(number % 4 == 0, named(packed, number // 4), named(ordinary, number - number // 4 - 1))
    mixed = jax.random.permutation(jax.random.fold_in(own, 3), amount)
    donor, sink = mixed[0:amount // 2 * 2:2], mixed[1:amount // 2 * 2:2]
    room = jnp.minimum(lengths[donor] - 1, bound - lengths[sink]) // 2
    room = jnp.where((donor == sequence[0]) | (sink == sequence[0]) | (lengths[sink] == 0), 0, jnp.maximum(room, 0))
    moved = jax.random.randint(jax.random.fold_in(own, 4), (amount // 2,), 0, 1 << 20) % (room + 1)
    lengths = lengths.at[donor].add(-moved).at[sink].add(moved)
    items = jnp.searchsorted(jnp.cumsum(lengths), jnp.arange(rows * top), side="right").astype(jnp.int32)
    grid = items.reshape(top, rows).T
    grid = grid[jax.random.permutation(jax.random.fold_in(own, 1), rows)]
    turn = jax.random.randint(jax.random.fold_in(own, 2), (rows, 1), 0, top)
    return jnp.take_along_axis(grid, (jnp.arange(top)[None, :] + turn) % top, axis=1)


def shares(amount, total, reach, skew, full):
    weights = [(1 << 20) // math.isqrt(standing ** skew) + 1 for standing in range(1, amount + 1)]
    largest = reach if full else min(reach, max(-(-total // amount), total * weights[0] // sum(weights)))
    least = 1 if total - largest >= amount - 1 else 0
    given, rest = [largest] + [least] * (amount - 1), total - largest - least * (amount - 1)
    while rest > 0:
        movable = [i for i in range(1, amount) if given[i] < largest] or [i for i in range(1, amount) if given[i] < reach]
        whole, left = sum([weights[i] for i in movable]), rest
        for i in movable:
            addition = min(reach - given[i], max(1, left * weights[i] // whole), rest)
            given[i] = given[i] + addition
            rest = rest - addition
    return np.array(given)


def gaussian(rng, dims, scale, limit, cuts=(), kind=jnp.bfloat16):
    level = block_levels(rng, dims, cuts, -0.22, 0.18) if cuts else 1.0
    array = jax.random.normal(rng, dims, jnp.float32) * scale * level
    return jnp.minimum(jnp.maximum(array, -limit), limit).astype(kind)


def setup_inputs(seed: int = 0) -> dict:
    keys = jax.random.split(jax.random.key(seed), 12)
    node_load = gaussian(keys[0], (LATERAL_COUNT, SCEN, HORIZON_TICKS, NODE), 1.0, 6.0, ((0, 16), (2, 16)))
    drive_map = gaussian(keys[1], (LATERAL_COUNT, NODE, STATE), NODE ** -0.5, 0.25, ((0, 16),))
    decay_rate = draw_decay_rate(jax.random.fold_in(keys[11], 71), 0)
    counts = touch_ends(jax.random.randint(keys[3], (LATERAL_COUNT,), STATE // 4, STATE + 1), jax.random.fold_in(keys[3], 1), STATE // 4, STATE).astype(jnp.int32)
    out_map = gaussian(keys[4], (LATERAL_COUNT, 2, STATE), STATE ** -0.5, 0.375, ((0, 16),), jnp.float32)
    area_of_keys = jax.random.split(jax.random.fold_in(keys[5], 1), LATERAL_COUNT // FEED_DEV)
    area_of_turns = jax.random.permutation(jax.random.fold_in(keys[5], 3), LATERAL_COUNT // FEED_DEV)
    area_of = jax.vmap(lambda own, number: shared_out(jax.random.fold_in(keys[5], 2), own, number, FEED_DEV, AREAS, 1, CAP, 2))(area_of_keys, area_of_turns).reshape((LATERAL_COUNT, 1))
    head_bus = touch_ends(jax.random.randint(keys[6], (LATERAL_COUNT,), 0, BUS), jax.random.fold_in(keys[6], 1), 0, BUS - 1).astype(jnp.int32)
    rule_of = touch_ends(jax.random.randint(keys[7], (LATERAL_COUNT,), 0, RULES), jax.random.fold_in(keys[7], 1), 0, RULES - 1).astype(jnp.int32)
    rule_knots = draw_rule_knots(jax.random.fold_in(keys[11], 71), 0)
    levels = touch_ends(jax.random.randint(keys[9], (RULES, KNOTS), -1000, 1001), jax.random.fold_in(keys[9], 1), -1000, 1000).astype(jnp.int32)
    sensitivity = gaussian(keys[10], (AREAS, 2, BUS, BUS), 0.1, 0.6, ((0, 16),), jnp.float32)
    return dict(node_load=node_load, drive_map=drive_map, decay_rate=decay_rate, counts=counts, out_map=out_map, area_of=area_of, head_bus=head_bus, rule_of=rule_of, rule_knots=rule_knots, levels=levels, sensitivity=sensitivity)


def setpoint_rule(volts, knot_volts, knot_levels):
    result = knot_levels[:, 0:1] + jnp.zeros_like(volts)
    for piece in range(knot_volts.shape[1] - 1):
        span_width = knot_volts[:, piece + 1:piece + 2] - knot_volts[:, piece:piece + 1]
        slope = (knot_levels[:, piece + 1:piece + 2] - knot_levels[:, piece:piece + 1]) / span_width
        result = result + slope * jnp.clip(volts - knot_volts[:, piece:piece + 1], 0.0, span_width)
    return result


def reference(node_load, drive_map, decay_rate, counts, out_map, area_of, head_bus, rule_of, rule_knots, levels, sensitivity):
    state_ids = jnp.arange(STATE, dtype=jnp.int32)

    def feeder_run(inputs):
        loads, mapping, retain, live_count, output_mapping = inputs
        live = (state_ids < live_count).astype(jnp.float32)
        drive = jnp.einsum('ctn,ns->cts', loads.astype(jnp.float32), mapping.astype(jnp.float32), precision=lax.Precision.HIGHEST) * live

        def advance(current, pair):
            keep, push = pair
            current = keep[None, :] * current + push
            return current, current

        _, history_record = lax.scan(advance, jnp.zeros((SCEN, STATE), jnp.float32), (retain, jnp.swapaxes(drive, 0, 1)))
        flow_value = jnp.einsum('dqp,up->udq', history_record, output_mapping, precision=lax.Precision.HIGHEST)
        return flow_value.reshape(2, HORIZON_TICKS * SCEN)

    head_flow = lax.map(feeder_run, (node_load, drive_map, decay_rate, counts, out_map))
    area_ids = area_of[:, 0]
    bus_hot = (head_bus[:, None] == jnp.arange(BUS, dtype=jnp.int32)[None, :]).astype(jnp.float32)

    def area_run(inputs):
        area_index, sens_block = inputs
        chosen = bus_hot * (area_ids == area_index).astype(jnp.float32)[:, None]
        bus_flow = jnp.einsum('fb,fkr->kbr', chosen, head_flow, precision=lax.Precision.HIGHEST)
        return jnp.einsum('kbe,ker->br', sens_block, bus_flow, precision=lax.Precision.HIGHEST)

    volt_shift = lax.map(area_run, (jnp.arange(AREAS, dtype=jnp.int32), sensitivity))
    volts = volt_shift[area_ids, head_bus]
    knot_volts = rule_knots.astype(jnp.float32)[rule_of] / 1000.0
    knot_levels = levels.astype(jnp.float32)[rule_of] / 1000.0
    settings = setpoint_rule(volts, knot_volts, knot_levels)
    return settings.reshape(LATERAL_COUNT, HORIZON_TICKS, SCEN)
```

```python
import functools

import jax
import jax.numpy as jnp
from jax import lax
from jax.experimental import pallas as pl
from jax.experimental.pallas import tpu as pltpu
from jax.sharding import PartitionSpec as P

F32 = jnp.float32
BF16 = jnp.bfloat16
CAP = 2
NT = (((1,), (1,)), ((), ()))
NN = (((1,), (0,)), ((), ()))
WHOLE = pl.BlockSpec(memory_space=pltpu.VMEM)
SCALARS = pl.BlockSpec(memory_space=pltpu.SMEM)


def split(x):
    high = x.astype(BF16)
    return high, (x - high.astype(F32)).astype(BF16)


def dot(a, b, dims):
    return lax.dot_general(a, b, dims, preferred_element_type=F32)


def dot3(a, b, dims):
    a_high, a_low = split(a)
    b_high, b_low = split(b)
    rows = a.shape[0]
    both = dot(jnp.concatenate([a_high, a_low], 0), b_high, dims)
    return both[:rows] + both[rows:] + dot(a_high, b_low, dims)


def member_slots(areas, block):
    lane = lax.broadcasted_iota(jnp.int32, areas.shape, 1)
    within = lax.rem(lane, block)
    rank = jnp.zeros_like(areas)
    for back in range(1, block):
        same = (areas == pltpu.roll(areas, back, 1)) & (within >= back)
        rank = rank + same.astype(jnp.int32)
    return lax.div(lane, block) * CAP + rank


def drive_kernel(
    counts_ref, load_ref, map_ref, decay_ref, out_ref, area_ref, bus_ref, sens_ref,
    send_ref, flow_ref, sens_out_ref,
):
    step = pl.program_id(0)
    span, scen, nodes = load_ref.shape[1:]
    width = map_ref.shape[2]
    per_dev = decay_ref.shape[1]

    drive = dot(load_ref[0].reshape(span * scen, nodes), map_ref[0], NN)
    live = lax.broadcasted_iota(jnp.int32, (1, width), 1) < counts_ref[step]
    drive = jnp.where(live, drive, 0.0)
    state = drive[:scen]
    states = [state]
    retain = [decay_ref[t, pl.ds(step, 1), :] for t in range(span)]
    for t in range(1, span):
        state = retain[t] * state + drive[t * scen : (t + 1) * scen]
        states.append(state)
    send_ref[0, 0:scen] = state
    tail = send_ref.shape[1] - scen
    send_ref[0, scen:] = jnp.concatenate(
        retain + [jnp.zeros((tail - span, width), F32)], 0
    )
    flow = dot3(out_ref[0], jnp.concatenate(states, 0), NT)
    lanes = flow_ref.shape[2]
    planes = flow.shape[1] // lanes
    for k in range(2):
        for piece in range(planes):
            flow_ref[k * planes + piece, pl.ds(step, 1), :] = flow[
                k : k + 1, piece * lanes : (piece + 1) * lanes
            ]

    @pl.when(step == 0)
    def _():
        areas = area_ref[...]
        buses = bus_ref[...]
        count = areas.shape[1]
        bus_count = sens_ref.shape[2]
        blocks = count // per_dev
        members = blocks * CAP
        slots = member_slots(areas, per_dev)
        mine = areas == lax.axis_index("feeder")
        bus_hot = (
            lax.broadcasted_iota(jnp.int32, (bus_count, count), 0) == buses
        ).astype(BF16)
        row = lax.broadcasted_iota(jnp.int32, (members, count), 0)
        wanted = jnp.where(row < blocks, row * CAP, (row - blocks) * CAP + 1)
        by_rank = ((wanted == slots) & mine).astype(BF16)
        by_slot = ((row == slots) & mine).astype(BF16)
        row_bus = dot(by_rank, bus_hot, NT).astype(BF16)
        column_bus = dot(by_slot, bus_hot, NT).astype(BF16)
        parts = []
        for k in range(2):
            sens = sens_ref[0, k]
            high, low = split(sens)
            picked = dot(row_bus, high, NN) + dot(row_bus, low, NN)
            high, low = split(picked)
            parts.append(dot(high, column_bus, NT) + dot(low, column_bus, NT))
        sens_out_ref[...] = jnp.concatenate(
            [parts[k][s * blocks : (s + 1) * blocks] for s in range(CAP) for k in range(2)], 1
        )


def owner_kernel(recv_ref, out_ref, back_ref):
    chunks, rows, width = recv_ref.shape
    scen = back_ref.shape[2] // 2
    span = 6
    me = lax.axis_index("tm")
    out = out_ref[me]
    state = recv_ref[0, 0:scen]
    back_ref[0] = jnp.zeros(back_ref.shape[1:], F32)
    for chunk in range(1, chunks):
        product = recv_ref[chunk, scen : scen + 1]
        kept = [product]
        for t in range(1, span):
            product = product * recv_ref[chunk, scen + t : scen + t + 1]
            kept.append(product)
        blank = jnp.zeros((2, width), F32)
        even = [out[k : k + 1] * kept[t] for k in range(2) for t in range(0, span, 2)]
        odd = [out[k : k + 1] * kept[t] for k in range(2) for t in range(1, span, 2)]
        weights = jnp.concatenate(even + [blank] + odd + [blank], 0)
        flow = dot3(weights, state, NT)
        back_ref[chunk] = jnp.concatenate([flow[:8], flow[8:]], 1)
        if chunk < chunks - 1:
            state = recv_ref[chunk, 0:scen] + product * state


def join_kernel(back_ref, flow_ref, sens_ref, all_ref):
    planes, per_dev, lanes = flow_ref.shape
    stride = back_ref.shape[0] // per_dev
    for plane in range(planes):
        all_ref[plane] = flow_ref[plane] + back_ref[pl.ds(plane, per_dev, stride=stride), :]
    all_ref[planes] = sens_ref[...]


def mix_kernel(
    area_s, rule_s, knots_ref, levels_ref, area_ref, every_ref, result_ref,
    picked_ref, knot_ref, level_ref, own_ref,
):
    blocks, planes, per_dev, lanes = every_ref.shape
    planes = planes - 1
    count = blocks * per_dev
    me = lax.axis_index("feeder")
    areas = area_ref[...]
    slots = member_slots(areas, per_dev)
    for f in range(per_dev):
        area = area_s[me * per_dev + f]
        rank = jnp.int32(0)
        for earlier in range(f):
            rank = rank + jnp.where(area_s[me * per_dev + earlier] == area, 1, 0)
        row = every_ref[area, planes, pl.ds(me, 1), :]
        lane = lax.broadcasted_iota(jnp.int32, (1, lanes), 1)
        picked_ref[f : f + 1, :] = jnp.where(
            lax.div(lane, lanes // CAP) == rank, row, 0.0
        )
        rule = rule_s[me * per_dev + f]
        knot_ref[f : f + 1, :] = knots_ref[pl.ds(rule, 1), :].astype(F32) / 1000.0
        level_ref[f : f + 1, :] = levels_ref[pl.ds(rule, 1), :].astype(F32) / 1000.0
        own_ref[f : f + 1, :] = (areas == area).astype(F32)
    members = blocks * CAP
    lane = lax.broadcasted_iota(jnp.int32, (per_dev, lanes), 1)
    of_k = lax.rem(lax.div(lane, members), 2)
    picked = picked_ref[...]
    picked = jnp.concatenate([jnp.where(of_k == k, picked, 0.0) for k in range(2)], 0)
    spread = (
        lax.rem(lax.broadcasted_iota(jnp.int32, (lanes, count), 0), members) == slots
    ).astype(BF16)
    high, low = split(picked)
    weight = dot(high, spread, NN) + dot(low, spread, NN)
    own = own_ref[...]
    knot_volts = knot_ref[...]
    knot_levels = level_ref[...]
    per_k = planes // 2
    scen = result_ref.shape[2]
    weights = [weight[k * per_dev : (k + 1) * per_dev] * own for k in range(2)]
    for piece in range(per_k):
        volts = sum(
            dot3(weights[k], every_ref[:, k * per_k + piece].reshape(count, lanes), NN)
            for k in range(2)
        )
        result = knot_levels[:, 0:1] + jnp.zeros_like(volts)
        for j in range(knot_volts.shape[1] - 1):
            span_width = knot_volts[:, j + 1 : j + 2] - knot_volts[:, j : j + 1]
            slope = (knot_levels[:, j + 1 : j + 2] - knot_levels[:, j : j + 1]) / span_width
            result = result + slope * jnp.minimum(
                jnp.maximum(volts - knot_volts[:, j : j + 1], 0.0), span_width
            )
        result_ref[2 * piece] = result[:, :scen]
        result_ref[2 * piece + 1] = result[:, scen:]


def per_device(
    node_load, drive_map, decay_rate, counts, out_map, area_of, head_bus, rule_of,
    rule_knots, levels, sensitivity,
):
    per_dev, scen, span, nodes = node_load.shape
    width = drive_map.shape[2]
    feeders = area_of.shape[0]
    chunks = lax.axis_size("tm")
    blocks = lax.axis_size("feeder")
    rows = scen + 8
    lanes = 2 * scen
    planes = span
    load = jnp.transpose(node_load, (0, 2, 1, 3))
    decay = jnp.transpose(decay_rate, (1, 0, 2))
    area_row = jnp.transpose(area_of, (1, 0))
    bus_row = head_bus.reshape(1, feeders)

    send, flow, sens = pl.pallas_call(
        drive_kernel,
        grid=(per_dev,),
        in_specs=[
            SCALARS,
            pl.BlockSpec((1, span, scen, nodes), lambda f: (f, 0, 0, 0)),
            pl.BlockSpec((1, nodes, width), lambda f: (f, 0, 0)),
            pl.BlockSpec((span, per_dev, width), lambda f: (0, 0, 0)),
            pl.BlockSpec((1, 2, width), lambda f: (f, 0, 0)),
            pl.BlockSpec((1, feeders), lambda f: (0, 0)),
            pl.BlockSpec((1, feeders), lambda f: (0, 0)),
            pl.BlockSpec(sensitivity.shape, lambda f: (0, 0, 0, 0)),
        ],
        out_specs=[
            pl.BlockSpec((1, rows, width), lambda f: (f, 0, 0)),
            pl.BlockSpec((planes, per_dev, lanes), lambda f: (0, 0, 0)),
            pl.BlockSpec((per_dev, lanes), lambda f: (0, 0)),
        ],
        out_shape=[
            jax.ShapeDtypeStruct((per_dev, rows, width), F32),
            jax.ShapeDtypeStruct((planes, per_dev, lanes), F32),
            jax.ShapeDtypeStruct((per_dev, lanes), F32),
        ],
        compiler_params=pltpu.CompilerParams(vmem_limit_bytes=32 * 1024 * 1024),
        name="drive",
    )(counts, load, drive_map, decay, out_map, area_row, bus_row, sensitivity)

    owned = lax.all_to_all(send, "tm", 0, 0, tiled=True)
    back = pl.pallas_call(
        owner_kernel,
        in_specs=[WHOLE, WHOLE],
        out_specs=WHOLE,
        out_shape=jax.ShapeDtypeStruct((chunks, 8, lanes), F32),
        compiler_params=pltpu.CompilerParams(vmem_limit_bytes=16 * 1024 * 1024),
        name="owner",
    )(owned, out_map)
    back = lax.all_to_all(back, "tm", 0, 0, tiled=True)
    joined = pl.pallas_call(
        join_kernel,
        in_specs=[WHOLE] * 3,
        out_specs=WHOLE,
        out_shape=jax.ShapeDtypeStruct((planes + 1, per_dev, lanes), F32),
        name="join",
    )(back.reshape(per_dev * 8, lanes), flow, sens)
    every = lax.all_gather(joined, "feeder", axis=0, tiled=False)
    result = pl.pallas_call(
        mix_kernel,
        in_specs=[SCALARS, SCALARS, WHOLE, WHOLE, WHOLE, WHOLE],
        out_specs=WHOLE,
        out_shape=jax.ShapeDtypeStruct((span, per_dev, scen), F32),
        scratch_shapes=[
            pltpu.VMEM((per_dev, lanes), F32),
            pltpu.VMEM((per_dev, rule_knots.shape[1]), F32),
            pltpu.VMEM((per_dev, rule_knots.shape[1]), F32),
            pltpu.VMEM((per_dev, feeders), F32),
        ],
        compiler_params=pltpu.CompilerParams(vmem_limit_bytes=16 * 1024 * 1024),
        name="mix",
    )(area_of.reshape(feeders), rule_of, rule_knots, levels, area_row, every)
    return jnp.transpose(result, (1, 0, 2))


def solution(mesh):
    return jax.shard_map(
        per_device,
        mesh=mesh,
        in_specs=(
            P("feeder", None, "tm", None),
            P("feeder", None, None),
            P("feeder", "tm", None),
            P("feeder"),
            P("feeder", None, None),
            P(),
            P(),
            P(),
            P(),
            P(),
            P("feeder", None, None, None),
        ),
        out_specs=P("feeder", "tm", None),
        check_vma=False,
    )
```

```python
import functools

import jax
import jax.numpy as jnp
from jax import lax
from jax.experimental import pallas as pl
from jax.experimental.pallas import tpu as pltpu
from jax.sharding import PartitionSpec as P

F32 = jnp.float32
BF16 = jnp.bfloat16
CAP = 2
GROUPS = (4, 4, 4, 4)
NT = (((1,), (1,)), ((), ()))
NN = (((1,), (0,)), ((), ()))
WHOLE = pl.BlockSpec(memory_space=pltpu.VMEM)
SCALARS = pl.BlockSpec(memory_space=pltpu.SMEM)


def split(x):
    high = x.astype(BF16)
    return high, (x - high.astype(F32)).astype(BF16)


def dot(a, b, dims):
    return lax.dot_general(a, b, dims, preferred_element_type=F32)


def dot3(a, b, dims):
    a_high, a_low = split(a)
    b_high, b_low = split(b)
    rows = a.shape[0]
    both = dot(jnp.concatenate([a_high, a_low], 0), b_high, dims)
    return both[:rows] + both[rows:] + dot(a_high, b_low, dims)


def member_slots(areas, block):
    lane = lax.broadcasted_iota(jnp.int32, areas.shape, 1)
    within = lax.rem(lane, block)
    rank = jnp.zeros_like(areas)
    for back in range(1, block):
        same = (areas == pltpu.roll(areas, back, 1)) & (within >= back)
        rank = rank + same.astype(jnp.int32)
    return lax.div(lane, block) * CAP + rank


def area_matrix(areas, buses, sens_ref, per_dev):
    count = areas.shape[1]
    bus_count = sens_ref.shape[2]
    blocks = count // per_dev
    members = blocks * CAP
    slots = member_slots(areas, per_dev)
    mine = areas == lax.axis_index("feeder")
    bus_hot = (lax.broadcasted_iota(jnp.int32, (bus_count, count), 0) == buses).astype(BF16)
    row = lax.broadcasted_iota(jnp.int32, (members, count), 0)
    wanted = jnp.where(row < blocks, row * CAP, (row - blocks) * CAP + 1)
    by_rank = ((wanted == slots) & mine).astype(BF16)
    by_slot = ((row == slots) & mine).astype(BF16)
    row_bus = dot(by_rank, bus_hot, NT).astype(BF16)
    column_bus = dot(by_slot, bus_hot, NT).astype(BF16)
    parts = []
    for k in range(2):
        high, low = split(sens_ref[0, k])
        picked = dot(row_bus, high, NN) + dot(row_bus, low, NN)
        high, low = split(picked)
        parts.append(dot(high, column_bus, NT) + dot(low, column_bus, NT))
    return jnp.concatenate(
        [parts[k][s * blocks : (s + 1) * blocks] for s in range(CAP) for k in range(2)], 1
    )


def drive_kernel(
    counts_hbm, load_hbm, map_hbm, decay_hbm, out_hbm, area_hbm, bus_hbm, sens_hbm,
    send_hbm, flow_ref, sens_out_ref,
    send_ref, counts_ref, load_ref, map_ref, decay_ref, out_ref, area_ref, bus_ref, sens_ref,
    load_sems, map_sems, send_sems, sems,
):
    per_dev, span, scen, nodes = load_ref.shape
    width = map_ref.shape[2]
    lanes = flow_ref.shape[2]
    small = [
        pltpu.make_async_copy(source, target, sems.at[i])
        for i, (source, target) in enumerate(
            [
                (area_hbm, area_ref),
                (bus_hbm, bus_ref),
                (sens_hbm, sens_ref),
                (counts_hbm, counts_ref),
                (decay_hbm, decay_ref),
                (out_hbm, out_ref),
            ]
        )
    ]
    loads = [
        pltpu.make_async_copy(load_hbm.at[f], load_ref.at[f], load_sems.at[f])
        for f in range(per_dev)
    ]
    maps = [
        pltpu.make_async_copy(map_hbm.at[f], map_ref.at[f], map_sems.at[f])
        for f in range(per_dev)
    ]
    for copy in small:
        copy.start()
    for f in range(per_dev):
        loads[f].start(priority=0)
        maps[f].start(priority=1)
    for copy in small:
        copy.wait()
    sens_out_ref[...] = area_matrix(area_ref[...], bus_ref[...], sens_ref, per_dev)
    blank = jnp.zeros((send_ref.shape[1] - scen - span, width), F32)
    lane = lax.broadcasted_iota(jnp.int32, (1, width), 1)
    sends = [
        pltpu.make_async_copy(send_ref.at[f], send_hbm.at[f], send_sems.at[f])
        for f in range(per_dev)
    ]

    def record(f, drive):
        drive = jnp.where(lane < counts_ref[f], drive, 0.0)
        retain = [decay_ref[t, f : f + 1, :] for t in range(span)]
        state = drive[:scen]
        states = [state]
        for t in range(1, span):
            state = retain[t] * state + drive[t * scen : (t + 1) * scen]
            states.append(state)
        send_ref[f, 0:scen] = state
        send_ref[f, scen:] = jnp.concatenate(retain + [blank], 0)
        return jnp.concatenate(states, 0)

    def project(f, states):
        flow = dot3(out_ref[f], states, NT)
        planes = flow.shape[1] // lanes
        for k in range(2):
            for piece in range(planes):
                flow_ref[k * planes + piece, f : f + 1, :] = flow[
                    k : k + 1, piece * lanes : (piece + 1) * lanes
                ]

    groups, begin = [], 0
    for size in GROUPS:
        groups.append(range(begin, begin + size))
        begin += size
    before, drives = [], []
    for group in groups + [[]]:
        for f in group:
            maps[f].wait()
            loads[f].wait()
        fresh = [
            dot(load_ref[f].reshape(span * scen, nodes), map_ref[f], NN) for f in group
        ]
        histories = [record(f, drive) for f, drive in zip(before, drives)]
        for f, history in zip(before, histories):
            project(f, history)
        for f in before:
            sends[f].start()
        before, drives = group, fresh
    for copy in sends:
        copy.wait()


def owner_kernel(recv_ref, out_ref, back_ref):
    chunks, rows, width = recv_ref.shape
    scen = back_ref.shape[2] // 2
    span = 6
    me = lax.axis_index("tm")
    out = out_ref[me]
    state = recv_ref[0, 0:scen]
    back_ref[0] = jnp.zeros(back_ref.shape[1:], F32)
    for chunk in range(1, chunks):
        product = recv_ref[chunk, scen : scen + 1]
        kept = [product]
        for t in range(1, span):
            product = product * recv_ref[chunk, scen + t : scen + t + 1]
            kept.append(product)
        blank = jnp.zeros((2, width), F32)
        even = [out[k : k + 1] * kept[t] for k in range(2) for t in range(0, span, 2)]
        odd = [out[k : k + 1] * kept[t] for k in range(2) for t in range(1, span, 2)]
        weights = jnp.concatenate(even + [blank] + odd + [blank], 0)
        flow = dot3(weights, state, NT)
        back_ref[chunk] = jnp.concatenate([flow[:8], flow[8:]], 1)
        if chunk < chunks - 1:
            state = recv_ref[chunk, 0:scen] + product * state


def join_kernel(back_ref, flow_ref, sens_ref, all_ref):
    planes, per_dev, lanes = flow_ref.shape
    stride = back_ref.shape[0] // per_dev
    for plane in range(planes):
        all_ref[plane] = flow_ref[plane] + back_ref[pl.ds(plane, per_dev, stride=stride), :]
    all_ref[planes] = sens_ref[...]


def mix_kernel(
    area_s, rule_s, knots_ref, levels_ref, area_ref, every_ref, result_ref,
    picked_ref, knot_ref, level_ref, own_ref,
):
    blocks, planes, per_dev, lanes = every_ref.shape
    planes = planes - 1
    count = blocks * per_dev
    me = lax.axis_index("feeder")
    areas = area_ref[...]
    slots = member_slots(areas, per_dev)
    for f in range(per_dev):
        area = area_s[me * per_dev + f]
        rank = jnp.int32(0)
        for earlier in range(f):
            rank = rank + jnp.where(area_s[me * per_dev + earlier] == area, 1, 0)
        row = every_ref[area, planes, pl.ds(me, 1), :]
        lane = lax.broadcasted_iota(jnp.int32, (1, lanes), 1)
        picked_ref[f : f + 1, :] = jnp.where(
            lax.div(lane, lanes // CAP) == rank, row, 0.0
        )
        rule = rule_s[me * per_dev + f]
        knot_ref[f : f + 1, :] = knots_ref[pl.ds(rule, 1), :].astype(F32) / 1000.0
        level_ref[f : f + 1, :] = levels_ref[pl.ds(rule, 1), :].astype(F32) / 1000.0
        own_ref[f : f + 1, :] = (areas == area).astype(F32)
    members = blocks * CAP
    lane = lax.broadcasted_iota(jnp.int32, (per_dev, lanes), 1)
    of_k = lax.rem(lax.div(lane, members), 2)
    picked = picked_ref[...]
    picked = jnp.concatenate([jnp.where(of_k == k, picked, 0.0) for k in range(2)], 0)
    spread = (
        lax.rem(lax.broadcasted_iota(jnp.int32, (lanes, count), 0), members) == slots
    ).astype(BF16)
    high, low = split(picked)
    weight = dot(high, spread, NN) + dot(low, spread, NN)
    own = own_ref[...]
    knot_volts = knot_ref[...]
    knot_levels = level_ref[...]
    per_k = planes // 2
    scen = result_ref.shape[2]
    weights = [weight[k * per_dev : (k + 1) * per_dev] * own for k in range(2)]
    for piece in range(per_k):
        volts = sum(
            dot3(weights[k], every_ref[:, k * per_k + piece].reshape(count, lanes), NN)
            for k in range(2)
        )
        result = knot_levels[:, 0:1] + jnp.zeros_like(volts)
        for j in range(knot_volts.shape[1] - 1):
            span_width = knot_volts[:, j + 1 : j + 2] - knot_volts[:, j : j + 1]
            slope = (knot_levels[:, j + 1 : j + 2] - knot_levels[:, j : j + 1]) / span_width
            result = result + slope * jnp.minimum(
                jnp.maximum(volts - knot_volts[:, j : j + 1], 0.0), span_width
            )
        result_ref[2 * piece] = result[:, :scen]
        result_ref[2 * piece + 1] = result[:, scen:]


def drive_call(counts, load, drive_map, decay, out_map, area_row, bus_row, sensitivity):
    per_dev, span, scen, _ = load.shape
    width = drive_map.shape[2]
    rows, lanes = scen + 8, 2 * scen
    operands = (load, drive_map, decay, out_map, area_row, bus_row, sensitivity)
    return pl.pallas_call(
        drive_kernel,
        in_specs=[pl.BlockSpec(memory_space=pl.ANY)] * (1 + len(operands)),
        out_specs=[pl.BlockSpec(memory_space=pl.ANY), WHOLE, WHOLE],
        out_shape=[
            jax.ShapeDtypeStruct((per_dev, rows, width), F32),
            jax.ShapeDtypeStruct((span, per_dev, lanes), F32),
            jax.ShapeDtypeStruct((per_dev, lanes), F32),
        ],
        scratch_shapes=[pltpu.VMEM((per_dev, rows, width), F32)]
        + [pltpu.SMEM(counts.shape, counts.dtype)]
        + [pltpu.VMEM(x.shape, x.dtype) for x in operands]
        + [
            pltpu.SemaphoreType.DMA((per_dev,)),
            pltpu.SemaphoreType.DMA((per_dev,)),
            pltpu.SemaphoreType.DMA((per_dev,)),
            pltpu.SemaphoreType.DMA((6,)),
        ],
        compiler_params=pltpu.CompilerParams(vmem_limit_bytes=60 * 1024 * 1024),
        name="drive",
    )(counts, *operands)


def per_device(
    node_load, drive_map, decay_rate, counts, out_map, area_of, head_bus, rule_of,
    rule_knots, levels, sensitivity,
):
    per_dev, scen, span, nodes = node_load.shape
    width = drive_map.shape[2]
    feeders = area_of.shape[0]
    chunks = lax.axis_size("tm")
    blocks = lax.axis_size("feeder")
    rows = scen + 8
    lanes = 2 * scen
    planes = span
    load = jnp.transpose(node_load, (0, 2, 1, 3))
    decay = jnp.transpose(decay_rate, (1, 0, 2))
    area_row = jnp.transpose(area_of, (1, 0))
    bus_row = head_bus.reshape(1, feeders)

    send, flow, sens = drive_call(
        counts, load, drive_map, decay, out_map, area_row, bus_row, sensitivity
    )
    owned = lax.all_to_all(send, "tm", 0, 0, tiled=True)
    back = pl.pallas_call(
        owner_kernel,
        in_specs=[WHOLE, WHOLE],
        out_specs=WHOLE,
        out_shape=jax.ShapeDtypeStruct((chunks, 8, lanes), F32),
        compiler_params=pltpu.CompilerParams(vmem_limit_bytes=16 * 1024 * 1024),
        name="owner",
    )(owned, out_map)
    back = lax.all_to_all(back, "tm", 0, 0, tiled=True)
    joined = pl.pallas_call(
        join_kernel,
        in_specs=[WHOLE] * 3,
        out_specs=WHOLE,
        out_shape=jax.ShapeDtypeStruct((planes + 1, per_dev, lanes), F32),
        compiler_params=pltpu.CompilerParams(vmem_limit_bytes=8 * 1024 * 1024),
        name="join",
    )(back.reshape(per_dev * 8, lanes), flow, sens)
    every = lax.all_gather(joined, "feeder", axis=0, tiled=False)
    result = pl.pallas_call(
        mix_kernel,
        in_specs=[SCALARS, SCALARS, WHOLE, WHOLE, WHOLE, WHOLE],
        out_specs=WHOLE,
        out_shape=jax.ShapeDtypeStruct((span, per_dev, scen), F32),
        scratch_shapes=[
            pltpu.VMEM((per_dev, lanes), F32),
            pltpu.VMEM((per_dev, rule_knots.shape[1]), F32),
            pltpu.VMEM((per_dev, rule_knots.shape[1]), F32),
            pltpu.VMEM((per_dev, feeders), F32),
        ],
        compiler_params=pltpu.CompilerParams(vmem_limit_bytes=16 * 1024 * 1024),
        name="mix",
    )(area_of.reshape(feeders), rule_of, rule_knots, levels, area_row, every)
    return jnp.transpose(result, (1, 0, 2))


def solution(mesh):
    return jax.shard_map(
        per_device,
        mesh=mesh,
        in_specs=(
            P("feeder", None, "tm", None),
            P("feeder", None, None),
            P("feeder", "tm", None),
            P("feeder"),
            P("feeder", None, None),
            P(),
            P(),
            P(),
            P(),
            P(),
            P("feeder", None, None, None),
        ),
        out_specs=P("feeder", "tm", None),
        check_vma=False,
    )
```

```python
import functools

import jax
import jax.numpy as jnp
from jax import lax
from jax.experimental import pallas as pl
from jax.experimental.pallas import tpu as pltpu
from jax.sharding import PartitionSpec as P

F32 = jnp.float32
BF16 = jnp.bfloat16
CAP = 2
OWN, MASKS, HOT, SLOT, KNOT, SLOPE = range(6)
GROUPS = (4, 4, 4, 4)
NT = (((1,), (1,)), ((), ()))
NN = (((1,), (0,)), ((), ()))
WHOLE = pl.BlockSpec(memory_space=pltpu.VMEM)
ANYWHERE = pl.BlockSpec(memory_space=pl.ANY)


def split(x):
    high = x.astype(BF16)
    return high, (x - high.astype(F32)).astype(BF16)


def dot(a, b, dims):
    return lax.dot_general(a, b, dims, preferred_element_type=F32)


def dot3(a, b, dims):
    a_high, a_low = split(a)
    b_high, b_low = split(b)
    rows = a.shape[0]
    both = dot(jnp.concatenate([a_high, a_low], 0), b_high, dims)
    return both[:rows] + both[rows:] + dot(a_high, b_low, dims)


def member_slots(areas, block):
    lane = lax.broadcasted_iota(jnp.int32, areas.shape, 1)
    within = lax.rem(lane, block)
    rank = jnp.zeros_like(areas)
    for back in range(1, block):
        same = (areas == pltpu.roll(areas, back, 1)) & (within >= back)
        rank = rank + same.astype(jnp.int32)
    return lax.div(lane, block) * CAP + rank, rank


def area_matrix(areas, slots, buses, sens_ref, per_dev):
    count = areas.shape[1]
    bus_count = sens_ref.shape[2]
    blocks = count // per_dev
    members = blocks * CAP
    mine = areas == lax.axis_index("feeder")
    bus_hot = (lax.broadcasted_iota(jnp.int32, (bus_count, count), 0) == buses).astype(BF16)
    row = lax.broadcasted_iota(jnp.int32, (members, count), 0)
    wanted = jnp.where(row < blocks, row * CAP, (row - blocks) * CAP + 1)
    by_rank = ((wanted == slots) & mine).astype(BF16)
    by_slot = ((row == slots) & mine).astype(BF16)
    row_bus = dot(by_rank, bus_hot, NT).astype(BF16)
    column_bus = dot(by_slot, bus_hot, NT).astype(BF16)
    parts = []
    for k in range(2):
        high, low = split(sens_ref[0, k])
        picked = dot(row_bus, high, NN) + dot(row_bus, low, NN)
        high, low = split(picked)
        parts.append(dot(high, column_bus, NT) + dot(low, column_bus, NT))
    return jnp.concatenate(
        [parts[k][s * blocks : (s + 1) * blocks] for s in range(CAP) for k in range(2)], 1
    )


def drives_of(group, load_ref, map_ref):
    per_dev, span, scen, nodes = load_ref.shape
    return [dot(load_ref[f].reshape(span * scen, nodes), map_ref[f], NN) for f in group]


def states_of(f, drive, live_count, decay_ref):
    span = decay_ref.shape[0]
    scen = drive.shape[0] // span
    lane = lax.broadcasted_iota(jnp.int32, (1, drive.shape[1]), 1)
    drive = jnp.where(lane < live_count, drive, 0.0)
    state = drive[:scen]
    states = [state]
    for t in range(1, span):
        state = decay_ref[t, f : f + 1, :] * state + drive[t * scen : (t + 1) * scen]
        states.append(state)
    return states


def started(pairs, sems):
    copies = [
        pltpu.make_async_copy(source, target, sems.at[i])
        for i, (source, target) in enumerate(pairs)
    ]
    for copy in copies:
        copy.start()
    return copies


def started_feeders(load_hbm, load_ref, load_sems, map_hbm, map_ref, map_sems):
    per_dev = load_ref.shape[0]
    loads = [
        pltpu.make_async_copy(load_hbm.at[f], load_ref.at[f], load_sems.at[f])
        for f in range(per_dev)
    ]
    maps = [
        pltpu.make_async_copy(map_hbm.at[f], map_ref.at[f], map_sems.at[f])
        for f in range(per_dev)
    ]
    for f in range(per_dev):
        loads[f].start(priority=0)
        maps[f].start(priority=1)
    return loads, maps


def groups_of(sizes):
    groups, begin = [], 0
    for size in sizes:
        groups.append(range(begin, begin + size))
        begin += size
    return groups


def drive_kernel(
    counts_hbm, load_hbm, map_hbm, decay_hbm,
    send_ref,
    counts_ref, load_ref, map_ref, decay_ref,
    load_sems, map_sems, sems,
):
    per_dev, span, scen, nodes = load_ref.shape
    width = map_ref.shape[2]
    small = started([(counts_hbm, counts_ref), (decay_hbm, decay_ref)], sems)
    loads, maps = started_feeders(load_hbm, load_ref, load_sems, map_hbm, map_ref, map_sems)
    for copy in small:
        copy.wait()
    blank = jnp.zeros((send_ref.shape[1] - scen - span, width), F32)
    before, drives = [], []
    for group in groups_of(GROUPS) + [[]]:
        for f in group:
            maps[f].wait()
            loads[f].wait()
        fresh = drives_of(group, load_ref, map_ref)
        for f, drive in zip(before, drives):
            send_ref[f, 0:scen] = states_of(f, drive, counts_ref[f], decay_ref)[-1]
            send_ref[f, scen:] = jnp.concatenate(
                [decay_ref[t, f : f + 1, :] for t in range(span)] + [blank], 0
            )
        before, drives = group, fresh


def side_kernel(
    counts_hbm, load_hbm, map_hbm, decay_hbm, out_hbm, area_ref, bus_ref, rule_ref, sens_hbm,
    knots_ref, levels_ref,
    flow_ref, table_ref,
    counts_ref, load_ref, map_ref, decay_ref, out_ref, sens_ref,
    load_sems, map_sems, sems,
):
    per_dev, span, scen, nodes = load_ref.shape
    lanes = flow_ref.shape[2]
    small = started(
        [
            (counts_hbm, counts_ref),
            (decay_hbm, decay_ref),
            (out_hbm, out_ref),
            (sens_hbm, sens_ref),
        ],
        sems,
    )
    loads, maps = started_feeders(load_hbm, load_ref, load_sems, map_hbm, map_ref, map_sems)
    areas = area_ref[...]
    rules = rule_ref[...]
    count = areas.shape[1]
    blocks = count // per_dev
    members = blocks * CAP
    slots, ranks = member_slots(areas, per_dev)
    me = lax.axis_index("feeder")
    feeder = lax.broadcasted_iota(jnp.int32, (per_dev, count), 1)
    here = feeder == me * per_dev + lax.broadcasted_iota(jnp.int32, (per_dev, count), 0)
    my_area = jnp.sum(jnp.where(here, areas, 0), axis=1, keepdims=True)
    my_rank = jnp.sum(jnp.where(here, ranks, 0), axis=1, keepdims=True)
    my_rule = jnp.sum(jnp.where(here, rules, 0), axis=1, keepdims=True)
    choice = lax.broadcasted_iota(jnp.int32, (per_dev, blocks), 1)
    hot = (choice == my_area).astype(F32)
    own = (areas == my_area).astype(F32)
    lane = lax.broadcasted_iota(jnp.int32, (per_dev, lanes), 1)
    of_rank = lax.div(lane, lanes // CAP) == my_rank
    of_k = lax.rem(lax.div(lane, members), 2)
    masks = [(of_rank & (of_k == k)).astype(F32) for k in range(2)]
    rule_count = knots_ref.shape[1]
    rule_choice = lax.broadcasted_iota(jnp.int32, (per_dev, rule_count), 1)
    rule_hot = (rule_choice == my_rule).astype(BF16)
    knots = knots_ref.shape[0]

    def looked_up(table_ref):
        high, low = split(table_ref[...].astype(F32))
        return (dot(rule_hot, high, NT) + dot(rule_hot, low, NT)) / 1000.0

    knot_volts = looked_up(knots_ref)
    knot_levels = looked_up(levels_ref)
    width = knot_volts[:, 1:] - knot_volts[:, : knots - 1]
    slope = (knot_levels[:, 1:] - knot_levels[:, : knots - 1]) / width
    table_ref[OWN, :, :] = own
    for k in range(2):
        table_ref[MASKS, :, k * lanes : (k + 1) * lanes] = masks[k]
    table_ref[HOT, :, :blocks] = hot
    table_ref[SLOT, :, :] = slots.astype(F32) + jnp.zeros((per_dev, count), F32)
    table_ref[KNOT, :, :knots] = knot_volts
    table_ref[KNOT, :, lanes : lanes + 1] = knot_levels[:, 0:1]
    table_ref[SLOPE, :, : knots - 1] = width
    table_ref[SLOPE, :, lanes : lanes + knots - 1] = slope
    for copy in small:
        copy.wait()
    planes = flow_ref.shape[0] - 1
    flow_ref[planes] = area_matrix(areas, slots, bus_ref[...], sens_ref, per_dev)
    for group in groups_of(GROUPS):
        for f in group:
            maps[f].wait()
            loads[f].wait()
        drives = drives_of(group, load_ref, map_ref)
        histories = [
            states_of(f, drive, counts_ref[f], decay_ref) for f, drive in zip(group, drives)
        ]
        for f, history in zip(group, histories):
            flow = dot3(out_ref[f], jnp.concatenate(history, 0), NT)
            for k in range(2):
                for piece in range(planes // 2):
                    flow_ref[k * (planes // 2) + piece, f : f + 1, :] = flow[
                        k : k + 1, piece * lanes : (piece + 1) * lanes
                    ]


def owner_kernel(recv_ref, out_ref, back_ref):
    chunks, rows, width = recv_ref.shape
    scen = back_ref.shape[2] // 2
    span = 6
    me = lax.axis_index("tm")
    out = out_ref[me]
    state = recv_ref[0, 0:scen]
    back_ref[0] = jnp.zeros(back_ref.shape[1:], F32)
    for chunk in range(1, chunks):
        product = recv_ref[chunk, scen : scen + 1]
        kept = [product]
        for t in range(1, span):
            product = product * recv_ref[chunk, scen + t : scen + t + 1]
            kept.append(product)
        blank = jnp.zeros((2, width), F32)
        even = [out[k : k + 1] * kept[t] for k in range(2) for t in range(0, span, 2)]
        odd = [out[k : k + 1] * kept[t] for k in range(2) for t in range(1, span, 2)]
        weights = jnp.concatenate(even + [blank] + odd + [blank], 0)
        flow = dot3(weights, state, NT)
        back_ref[chunk] = jnp.concatenate([flow[:8], flow[8:]], 1)
        if chunk < chunks - 1:
            state = recv_ref[chunk, 0:scen] + product * state


def join_kernel(back_ref, flow_ref, all_ref):
    planes, per_dev, lanes = flow_ref.shape
    stride = back_ref.shape[0] // per_dev
    for plane in range(planes - 1):
        all_ref[plane] = flow_ref[plane] + back_ref[pl.ds(plane, per_dev, stride=stride), :]
    all_ref[planes - 1] = flow_ref[planes - 1]


def mix_kernel(knots, table_ref, every_ref, result_ref):
    blocks, planes, per_dev, lanes = every_ref.shape
    planes = planes - 1
    count = blocks * per_dev
    members = blocks * CAP
    me = lax.axis_index("feeder")
    hot = table_ref[HOT, :, :blocks].astype(BF16)
    masks = [
        table_ref[MASKS, :, k * lanes : (k + 1) * lanes].astype(BF16) for k in range(2)
    ]
    row = lax.rem(lax.broadcasted_iota(jnp.int32, (lanes, count), 0), members)
    spread = (row.astype(F32) == table_ref[SLOT, 0:1, :]).astype(BF16)
    high, low = split(every_ref[:, planes, pl.ds(me, 1), :].reshape(blocks, lanes))
    weight = jnp.zeros((2 * per_dev, count), F32)
    for part in (high, low):
        picked = dot(hot, part, NN).astype(BF16)
        weight = weight + dot(
            jnp.concatenate([picked * masks[0], picked * masks[1]], 0), spread, NN
        )
    own = table_ref[OWN]
    weights = [weight[k * per_dev : (k + 1) * per_dev] * own for k in range(2)]
    per_k = planes // 2
    scen = result_ref.shape[2]
    knot_volts = table_ref[KNOT, :, :knots]
    first = table_ref[KNOT, :, lanes : lanes + 1]
    widths = table_ref[SLOPE, :, : knots - 1]
    slopes = table_ref[SLOPE, :, lanes : lanes + knots - 1]
    for piece in range(per_k):
        volts = sum(
            dot3(weights[k], every_ref[:, k * per_k + piece].reshape(count, lanes), NN)
            for k in range(2)
        )
        result = first + jnp.zeros_like(volts)
        for j in range(knots - 1):
            result = result + slopes[:, j : j + 1] * jnp.minimum(
                jnp.maximum(volts - knot_volts[:, j : j + 1], 0.0), widths[:, j : j + 1]
            )
        result_ref[2 * piece] = result[:, :scen]
        result_ref[2 * piece + 1] = result[:, scen:]


def drive_call(counts, load, drive_map, decay):
    per_dev, span, scen, _ = load.shape
    width = drive_map.shape[2]
    rows = scen + 8
    operands = (load, drive_map, decay)
    return pl.pallas_call(
        drive_kernel,
        in_specs=[ANYWHERE] * 4,
        out_specs=WHOLE,
        out_shape=pltpu.VMEM((per_dev, rows, width), F32),
        scratch_shapes=[pltpu.SMEM(counts.shape, counts.dtype)]
        + [pltpu.VMEM(x.shape, x.dtype) for x in operands]
        + [pltpu.SemaphoreType.DMA((per_dev,))] * 2
        + [pltpu.SemaphoreType.DMA((2,))],
        compiler_params=pltpu.CompilerParams(vmem_limit_bytes=58 * 1024 * 1024),
        name="drive",
    )(counts, *operands)


def side_call(
    counts, load, drive_map, decay, out_map, area_row, bus_row, rule_row, sensitivity,
    knots, levels,
):
    per_dev, span, scen, nodes = load.shape
    width = drive_map.shape[2]
    lanes = 2 * scen
    count = area_row.shape[1]
    shapes = [(span + 1, per_dev, lanes), (6, per_dev, count)]
    copied = (load, drive_map, decay, out_map, sensitivity)
    return pl.pallas_call(
        side_kernel,
        in_specs=[ANYWHERE] * 5 + [WHOLE] * 3 + [ANYWHERE] + [WHOLE] * 2,
        out_specs=[WHOLE] * len(shapes),
        out_shape=[pltpu.VMEM(shape, F32) for shape in shapes],
        scratch_shapes=[pltpu.SMEM(counts.shape, counts.dtype)]
        + [pltpu.VMEM(x.shape, x.dtype) for x in copied]
        + [pltpu.SemaphoreType.DMA((per_dev,))] * 2
        + [pltpu.SemaphoreType.DMA((4,))],
        compiler_params=pltpu.CompilerParams(vmem_limit_bytes=56 * 1024 * 1024),
        cost_estimate=pl.CostEstimate(
            flops=2 * per_dev * span * scen * nodes * width,
            bytes_accessed=20 * 1024 * 1024,
            transcendentals=0,
        ),
        name="side",
    )(
        counts, load, drive_map, decay, out_map, area_row, bus_row, rule_row, sensitivity,
        knots, levels,
    )


def per_device(
    node_load, drive_map, decay_rate, counts, out_map, area_of, head_bus, rule_of,
    rule_knots, levels, sensitivity,
):
    per_dev, scen, span, nodes = node_load.shape
    feeders = area_of.shape[0]
    chunks = lax.axis_size("tm")
    lanes = 2 * scen
    load = jnp.transpose(node_load, (0, 2, 1, 3))
    decay = jnp.transpose(decay_rate, (1, 0, 2))

    send = drive_call(counts, load, drive_map, decay)
    owned = lax.all_to_all(send, "tm", 0, 0, tiled=True)
    flow, table = side_call(
        counts, load, drive_map, decay, out_map,
        jnp.transpose(area_of, (1, 0)), head_bus.reshape(1, feeders),
        rule_of.reshape(1, feeders), sensitivity,
        jnp.transpose(rule_knots, (1, 0)), jnp.transpose(levels, (1, 0)),
    )
    owned, flow, table = lax.optimization_barrier((owned, flow, table))
    back = pl.pallas_call(
        owner_kernel,
        in_specs=[WHOLE, WHOLE],
        out_specs=WHOLE,
        out_shape=pltpu.VMEM((chunks, 8, lanes), F32),
        compiler_params=pltpu.CompilerParams(vmem_limit_bytes=16 * 1024 * 1024),
        name="owner",
    )(owned, out_map)
    back = lax.all_to_all(back, "tm", 0, 0, tiled=True)
    joined = pl.pallas_call(
        join_kernel,
        in_specs=[WHOLE] * 2,
        out_specs=WHOLE,
        out_shape=pltpu.VMEM(flow.shape, F32),
        compiler_params=pltpu.CompilerParams(vmem_limit_bytes=8 * 1024 * 1024),
        name="join",
    )(back.reshape(per_dev * 8, lanes), flow)
    every = lax.all_gather(joined, "feeder", axis=0, tiled=False)
    result = pl.pallas_call(
        functools.partial(mix_kernel, levels.shape[1]),
        in_specs=[WHOLE] * 2,
        out_specs=WHOLE,
        out_shape=jax.ShapeDtypeStruct((span, per_dev, scen), F32),
        compiler_params=pltpu.CompilerParams(vmem_limit_bytes=16 * 1024 * 1024),
        name="mix",
    )(table, every)
    return jnp.transpose(result, (1, 0, 2))


def solution(mesh):
    return jax.shard_map(
        per_device,
        mesh=mesh,
        in_specs=(
            P("feeder", None, "tm", None),
            P("feeder", None, None),
            P("feeder", "tm", None),
            P("feeder"),
            P("feeder", None, None),
            P(),
            P(),
            P(),
            P(),
            P(),
            P("feeder", None, None, None),
        ),
        out_specs=P("feeder", "tm", None),
        check_vma=False,
    )
```

```python
import functools

import jax
import jax.numpy as jnp
from jax import lax
from jax.experimental import pallas as pl
from jax.experimental.pallas import tpu as pltpu
from jax.sharding import PartitionSpec as P

F32 = jnp.float32
BF16 = jnp.bfloat16
CAP = 2
OWN, MASKS, HOT, SLOT, KNOT, SLOPE = range(6)
GROUPS = (6, 6, 4)
NT = (((1,), (1,)), ((), ()))
NN = (((1,), (0,)), ((), ()))
WHOLE = pl.BlockSpec(memory_space=pltpu.VMEM)
ANYWHERE = pl.BlockSpec(memory_space=pl.ANY)


def split(x):
    high = x.astype(BF16)
    return high, (x - high.astype(F32)).astype(BF16)


def dot(a, b, dims):
    return lax.dot_general(a, b, dims, preferred_element_type=F32)


def dot3(a, b, dims):
    a_high, a_low = split(a)
    b_high, b_low = split(b)
    rows = a.shape[0]
    both = dot(jnp.concatenate([a_high, a_low], 0), b_high, dims)
    return both[:rows] + both[rows:] + dot(a_high, b_low, dims)


def member_slots(areas, block):
    lane = lax.broadcasted_iota(jnp.int32, areas.shape, 1)
    within = lax.rem(lane, block)
    rank = jnp.zeros_like(areas)
    for back in range(1, block):
        same = (areas == pltpu.roll(areas, back, 1)) & (within >= back)
        rank = rank + same.astype(jnp.int32)
    return lax.div(lane, block) * CAP + rank, rank


def area_matrix(areas, slots, buses, sens_ref, per_dev):
    count = areas.shape[1]
    bus_count = sens_ref.shape[2]
    blocks = count // per_dev
    members = blocks * CAP
    mine = areas == lax.axis_index("feeder")
    bus_hot = (lax.broadcasted_iota(jnp.int32, (bus_count, count), 0) == buses).astype(BF16)
    row = lax.broadcasted_iota(jnp.int32, (members, count), 0)
    wanted = jnp.where(row < blocks, row * CAP, (row - blocks) * CAP + 1)
    by_rank = ((wanted == slots) & mine).astype(BF16)
    by_slot = ((row == slots) & mine).astype(BF16)
    row_bus = dot(by_rank, bus_hot, NT).astype(BF16)
    column_bus = dot(by_slot, bus_hot, NT).astype(BF16)
    parts = []
    for k in range(2):
        high, low = split(sens_ref[0, k])
        picked = dot(row_bus, high, NN) + dot(row_bus, low, NN)
        high, low = split(picked)
        parts.append(dot(high, column_bus, NT) + dot(low, column_bus, NT))
    return jnp.concatenate(
        [parts[k][s * blocks : (s + 1) * blocks] for s in range(CAP) for k in range(2)], 1
    )


def drives_of(group, load_ref, map_ref):
    per_dev, span, scen, nodes = load_ref.shape
    return [dot(load_ref[f].reshape(span * scen, nodes), map_ref[f], NN) for f in group]


def states_of(f, drive, decay_ref):
    span = decay_ref.shape[0]
    scen = drive.shape[0] // span
    state = drive[:scen]
    states = [state]
    for t in range(1, span):
        state = decay_ref[t, f : f + 1, :] * state + drive[t * scen : (t + 1) * scen]
        states.append(state)
    return states


def started(pairs, sems):
    copies = [
        pltpu.make_async_copy(source, target, sems.at[i])
        for i, (source, target) in enumerate(pairs)
    ]
    for copy in copies:
        copy.start()
    return copies


def started_feeders(load_hbm, load_ref, load_sems, map_hbm, map_ref, map_sems):
    per_dev = load_ref.shape[0]
    loads = [
        pltpu.make_async_copy(load_hbm.at[f], load_ref.at[f], load_sems.at[f])
        for f in range(per_dev)
    ]
    maps = [
        pltpu.make_async_copy(map_hbm.at[f], map_ref.at[f], map_sems.at[f])
        for f in range(per_dev)
    ]
    for f in range(per_dev):
        loads[f].start(priority=0)
        maps[f].start(priority=1)
    return loads, maps


def groups_of(sizes):
    groups, begin = [], 0
    for size in sizes:
        groups.append(range(begin, begin + size))
        begin += size
    return groups


def drive_kernel(
    counts_hbm, load_hbm, map_hbm, decay_hbm,
    send_hbm,
    send_ref, counts_ref, load_ref, map_ref, decay_ref,
    load_sems, map_sems, send_sems, sems,
):
    per_dev, span, scen, nodes = load_ref.shape
    width = map_ref.shape[2]
    small = started([(counts_hbm, counts_ref), (decay_hbm, decay_ref)], sems)
    loads, maps = started_feeders(load_hbm, load_ref, load_sems, map_hbm, map_ref, map_sems)
    for copy in small:
        copy.wait()
    blank = jnp.zeros((send_ref.shape[1] - scen - span, width), F32)
    sends = [
        pltpu.make_async_copy(send_ref.at[f], send_hbm.at[f], send_sems.at[f])
        for f in range(per_dev)
    ]
    state_id = lax.broadcasted_iota(jnp.int32, (1, width), 1)
    for group in groups_of(GROUPS):
        for f in group:
            maps[f].wait()
            loads[f].wait()
        drives = drives_of(group, load_ref, map_ref)
        for f, drive in zip(group, drives):
            send_ref[f, 0:scen] = jnp.where(
                state_id < counts_ref[f], states_of(f, drive, decay_ref)[-1], 0.0
            )
            send_ref[f, scen:] = jnp.concatenate(
                [decay_ref[t, f : f + 1, :] for t in range(span)] + [blank], 0
            )
        for f in group:
            sends[f].start()
    for copy in sends:
        copy.wait()


def side_kernel(
    counts_hbm, load_hbm, map_hbm, decay_hbm, out_hbm, area_ref, bus_ref, rule_ref, sens_hbm,
    knots_ref, levels_ref,
    flow_ref, table_ref,
    counts_ref, load_ref, map_ref, decay_ref, out_ref, sens_ref,
    load_sems, map_sems, sems,
):
    per_dev, span, scen, nodes = load_ref.shape
    lanes = flow_ref.shape[2]
    small = started(
        [
            (counts_hbm, counts_ref),
            (decay_hbm, decay_ref),
            (out_hbm, out_ref),
            (sens_hbm, sens_ref),
        ],
        sems,
    )
    loads, maps = started_feeders(load_hbm, load_ref, load_sems, map_hbm, map_ref, map_sems)
    areas = area_ref[...]
    rules = rule_ref[...]
    count = areas.shape[1]
    blocks = count // per_dev
    members = blocks * CAP
    slots, ranks = member_slots(areas, per_dev)
    me = lax.axis_index("feeder")
    feeder = lax.broadcasted_iota(jnp.int32, (per_dev, count), 1)
    here = feeder == me * per_dev + lax.broadcasted_iota(jnp.int32, (per_dev, count), 0)
    my_area = jnp.sum(jnp.where(here, areas, 0), axis=1, keepdims=True)
    my_rank = jnp.sum(jnp.where(here, ranks, 0), axis=1, keepdims=True)
    my_rule = jnp.sum(jnp.where(here, rules, 0), axis=1, keepdims=True)
    choice = lax.broadcasted_iota(jnp.int32, (per_dev, blocks), 1)
    hot = (choice == my_area).astype(F32)
    own = (areas == my_area).astype(F32)
    lane = lax.broadcasted_iota(jnp.int32, (per_dev, lanes), 1)
    of_rank = lax.div(lane, lanes // CAP) == my_rank
    of_k = lax.rem(lax.div(lane, members), 2)
    masks = [(of_rank & (of_k == k)).astype(F32) for k in range(2)]
    rule_count = knots_ref.shape[1]
    rule_choice = lax.broadcasted_iota(jnp.int32, (per_dev, rule_count), 1)
    rule_hot = (rule_choice == my_rule).astype(BF16)
    knots = knots_ref.shape[0]

    def looked_up(table_ref):
        high, low = split(table_ref[...].astype(F32))
        return (dot(rule_hot, high, NT) + dot(rule_hot, low, NT)) / 1000.0

    knot_volts = looked_up(knots_ref)
    knot_levels = looked_up(levels_ref)
    width = knot_volts[:, 1:] - knot_volts[:, : knots - 1]
    slope = (knot_levels[:, 1:] - knot_levels[:, : knots - 1]) / width
    table_ref[OWN, :, :] = own
    for k in range(2):
        table_ref[MASKS, :, k * lanes : (k + 1) * lanes] = masks[k]
    table_ref[HOT, :, :blocks] = hot
    table_ref[SLOT, :, :] = slots.astype(F32) + jnp.zeros((per_dev, count), F32)
    table_ref[KNOT, :, :knots] = knot_volts
    table_ref[KNOT, :, lanes : lanes + 1] = knot_levels[:, 0:1]
    table_ref[SLOPE, :, : knots - 1] = width
    table_ref[SLOPE, :, lanes : lanes + knots - 1] = slope
    for copy in small:
        copy.wait()
    planes = flow_ref.shape[0] - 1
    flow_ref[planes] = area_matrix(areas, slots, bus_ref[...], sens_ref, per_dev)
    state_id = lax.broadcasted_iota(jnp.int32, (1, map_ref.shape[2]), 1)
    for group in groups_of(GROUPS):
        for f in group:
            maps[f].wait()
            loads[f].wait()
        drives = drives_of(group, load_ref, map_ref)
        histories = [states_of(f, drive, decay_ref) for f, drive in zip(group, drives)]
        for f, history in zip(group, histories):
            out = jnp.where(state_id < counts_ref[f], out_ref[f], 0.0)
            flow = dot3(out, jnp.concatenate(history, 0), NT)
            for k in range(2):
                for piece in range(planes // 2):
                    flow_ref[k * (planes // 2) + piece, f : f + 1, :] = flow[
                        k : k + 1, piece * lanes : (piece + 1) * lanes
                    ]


def owner_kernel(recv_ref, out_ref, back_ref):
    chunks, rows, width = recv_ref.shape
    scen = back_ref.shape[2] // 2
    span = 6
    me = lax.axis_index("tm")
    out = out_ref[me]
    state = recv_ref[0, 0:scen]
    back_ref[0] = jnp.zeros(back_ref.shape[1:], F32)
    for chunk in range(1, chunks):
        product = recv_ref[chunk, scen : scen + 1]
        kept = [product]
        for t in range(1, span):
            product = product * recv_ref[chunk, scen + t : scen + t + 1]
            kept.append(product)
        blank = jnp.zeros((2, width), F32)
        even = [out[k : k + 1] * kept[t] for k in range(2) for t in range(0, span, 2)]
        odd = [out[k : k + 1] * kept[t] for k in range(2) for t in range(1, span, 2)]
        weights = jnp.concatenate(even + [blank] + odd + [blank], 0)
        flow = dot3(weights, state, NT)
        back_ref[chunk] = jnp.concatenate([flow[:8], flow[8:]], 1)
        if chunk < chunks - 1:
            state = recv_ref[chunk, 0:scen] + product * state


def join_kernel(back_ref, flow_ref, all_ref):
    planes = flow_ref.shape[0] - 1
    for plane in range(planes):
        all_ref[plane] = flow_ref[plane] + back_ref[:, plane, :]
    all_ref[planes] = flow_ref[planes]


def mix_kernel(knots, table_ref, every_ref, result_ref):
    blocks, planes, per_dev, lanes = every_ref.shape
    planes = planes - 1
    count = blocks * per_dev
    members = blocks * CAP
    me = lax.axis_index("feeder")
    hot = table_ref[HOT, :, :blocks].astype(BF16)
    masks = [
        table_ref[MASKS, :, k * lanes : (k + 1) * lanes].astype(BF16) for k in range(2)
    ]
    row = lax.rem(lax.broadcasted_iota(jnp.int32, (lanes, count), 0), members)
    spread = (row.astype(F32) == table_ref[SLOT, 0:1, :]).astype(BF16)
    high, low = split(every_ref[:, planes, pl.ds(me, 1), :].reshape(blocks, lanes))
    weight = jnp.zeros((2 * per_dev, count), F32)
    for part in (high, low):
        picked = dot(hot, part, NN).astype(BF16)
        weight = weight + dot(
            jnp.concatenate([picked * masks[0], picked * masks[1]], 0), spread, NN
        )
    own = table_ref[OWN]
    weights = [weight[k * per_dev : (k + 1) * per_dev] * own for k in range(2)]
    per_k = planes // 2
    scen = result_ref.shape[2]
    knot_volts = table_ref[KNOT, :, :knots]
    first = table_ref[KNOT, :, lanes : lanes + 1]
    widths = table_ref[SLOPE, :, : knots - 1]
    slopes = table_ref[SLOPE, :, lanes : lanes + knots - 1]
    for piece in range(per_k):
        volts = sum(
            dot3(weights[k], every_ref[:, k * per_k + piece].reshape(count, lanes), NN)
            for k in range(2)
        )
        result = first + jnp.zeros_like(volts)
        for j in range(knots - 1):
            result = result + slopes[:, j : j + 1] * jnp.minimum(
                jnp.maximum(volts - knot_volts[:, j : j + 1], 0.0), widths[:, j : j + 1]
            )
        result_ref[2 * piece] = result[:, :scen]
        result_ref[2 * piece + 1] = result[:, scen:]


def drive_call(counts, load, drive_map, decay):
    per_dev, span, scen, _ = load.shape
    width = drive_map.shape[2]
    rows = scen + 8
    operands = (load, drive_map, decay)
    return pl.pallas_call(
        drive_kernel,
        in_specs=[ANYWHERE] * 4,
        out_specs=ANYWHERE,
        out_shape=jax.ShapeDtypeStruct((per_dev, rows, width), F32),
        scratch_shapes=[
            pltpu.VMEM((per_dev, rows, width), F32),
            pltpu.SMEM(counts.shape, counts.dtype),
        ]
        + [pltpu.VMEM(x.shape, x.dtype) for x in operands]
        + [pltpu.SemaphoreType.DMA((per_dev,))] * 3
        + [pltpu.SemaphoreType.DMA((2,))],
        compiler_params=pltpu.CompilerParams(vmem_limit_bytes=58 * 1024 * 1024),
        name="drive",
    )(counts, *operands)


def side_call(
    counts, load, drive_map, decay, out_map, area_row, bus_row, rule_row, sensitivity,
    knots, levels,
):
    per_dev, span, scen, nodes = load.shape
    width = drive_map.shape[2]
    lanes = 2 * scen
    count = area_row.shape[1]
    shapes = [(span + 1, per_dev, lanes), (6, per_dev, count)]
    copied = (load, drive_map, decay, out_map, sensitivity)
    return pl.pallas_call(
        side_kernel,
        in_specs=[ANYWHERE] * 5 + [WHOLE] * 3 + [ANYWHERE] + [WHOLE] * 2,
        out_specs=[WHOLE] * len(shapes),
        out_shape=[pltpu.VMEM(shape, F32) for shape in shapes],
        scratch_shapes=[pltpu.SMEM(counts.shape, counts.dtype)]
        + [pltpu.VMEM(x.shape, x.dtype) for x in copied]
        + [pltpu.SemaphoreType.DMA((per_dev,))] * 2
        + [pltpu.SemaphoreType.DMA((4,))],
        compiler_params=pltpu.CompilerParams(vmem_limit_bytes=56 * 1024 * 1024),
        cost_estimate=pl.CostEstimate(
            flops=2 * per_dev * span * scen * nodes * width,
            bytes_accessed=20 * 1024 * 1024,
            transcendentals=0,
        ),
        name="side",
    )(
        counts, load, drive_map, decay, out_map, area_row, bus_row, rule_row, sensitivity,
        knots, levels,
    )


def per_device(
    node_load, drive_map, decay_rate, counts, out_map, area_of, head_bus, rule_of,
    rule_knots, levels, sensitivity,
):
    per_dev, scen, span, nodes = node_load.shape
    feeders = area_of.shape[0]
    chunks = lax.axis_size("tm")
    lanes = 2 * scen
    load = jnp.transpose(node_load, (0, 2, 1, 3))
    decay = jnp.transpose(decay_rate, (1, 0, 2))

    send = drive_call(counts, load, drive_map, decay)
    owned = lax.all_to_all(send, "tm", 0, 0, tiled=True)
    flow, table = side_call(
        counts, load, drive_map, decay, out_map,
        jnp.transpose(area_of, (1, 0)), head_bus.reshape(1, feeders),
        rule_of.reshape(1, feeders), sensitivity,
        jnp.transpose(rule_knots, (1, 0)), jnp.transpose(levels, (1, 0)),
    )
    owned, flow, table = lax.optimization_barrier((owned, flow, table))
    back = pl.pallas_call(
        owner_kernel,
        in_specs=[WHOLE, WHOLE],
        out_specs=WHOLE,
        out_shape=pltpu.VMEM((chunks, 8, lanes), F32),
        compiler_params=pltpu.CompilerParams(vmem_limit_bytes=16 * 1024 * 1024),
        name="owner",
    )(owned, out_map)
    back = lax.all_to_all(back, "tm", 0, 0, tiled=True)
    joined = pl.pallas_call(
        join_kernel,
        in_specs=[WHOLE] * 2,
        out_specs=WHOLE,
        out_shape=pltpu.VMEM(flow.shape, F32),
        compiler_params=pltpu.CompilerParams(vmem_limit_bytes=8 * 1024 * 1024),
        name="join",
    )(back, flow)
    every = lax.all_gather(joined, "feeder", axis=0, tiled=False)
    result = pl.pallas_call(
        functools.partial(mix_kernel, levels.shape[1]),
        in_specs=[WHOLE] * 2,
        out_specs=WHOLE,
        out_shape=jax.ShapeDtypeStruct((span, per_dev, scen), F32),
        compiler_params=pltpu.CompilerParams(vmem_limit_bytes=16 * 1024 * 1024),
        name="mix",
    )(table, every)
    return jnp.transpose(result, (1, 0, 2))


def solution(mesh):
    return jax.shard_map(
        per_device,
        mesh=mesh,
        in_specs=(
            P("feeder", None, "tm", None),
            P("feeder", None, None),
            P("feeder", "tm", None),
            P("feeder"),
            P("feeder", None, None),
            P(),
            P(),
            P(),
            P(),
            P(),
            P("feeder", None, None, None),
        ),
        out_specs=P("feeder", "tm", None),
        check_vma=False,
    )
```

```python
import functools

import jax
import jax.numpy as jnp
from jax import lax
from jax.experimental import pallas as pl
from jax.experimental.pallas import tpu as pltpu
from jax.sharding import PartitionSpec as P

F32 = jnp.float32
BF16 = jnp.bfloat16
CAP = 2
OWN, MASKS, HOT, SLOT, KNOT, SLOPE = range(6)
GROUPS = (6, 6, 4)
NT = (((1,), (1,)), ((), ()))
NN = (((1,), (0,)), ((), ()))
WHOLE = pl.BlockSpec(memory_space=pltpu.VMEM)
ANYWHERE = pl.BlockSpec(memory_space=pl.ANY)


def split(x):
    high = x.astype(BF16)
    return high, (x - high.astype(F32)).astype(BF16)


def dot(a, b, dims):
    return lax.dot_general(a, b, dims, preferred_element_type=F32)


def dot3(a, b, dims):
    a_high, a_low = split(a)
    b_high, b_low = split(b)
    rows = a.shape[0]
    both = dot(jnp.concatenate([a_high, a_low], 0), b_high, dims)
    return both[:rows] + both[rows:] + dot(a_high, b_low, dims)


def member_slots(areas, block):
    lane = lax.broadcasted_iota(jnp.int32, areas.shape, 1)
    within = lax.rem(lane, block)
    rank = jnp.zeros_like(areas)
    for back in range(1, block):
        same = (areas == pltpu.roll(areas, back, 1)) & (within >= back)
        rank = rank + same.astype(jnp.int32)
    return lax.div(lane, block) * CAP + rank, rank


def area_matrix(areas, slots, buses, sens_ref, per_dev):
    count = areas.shape[1]
    bus_count = sens_ref.shape[2]
    blocks = count // per_dev
    members = blocks * CAP
    mine = areas == lax.axis_index("feeder")
    bus_hot = (lax.broadcasted_iota(jnp.int32, (bus_count, count), 0) == buses).astype(BF16)
    row = lax.broadcasted_iota(jnp.int32, (members, count), 0)
    wanted = jnp.where(row < blocks, row * CAP, (row - blocks) * CAP + 1)
    by_rank = ((wanted == slots) & mine).astype(BF16)
    by_slot = ((row == slots) & mine).astype(BF16)
    row_bus = dot(by_rank, bus_hot, NT).astype(BF16)
    column_bus = dot(by_slot, bus_hot, NT).astype(BF16)
    parts = []
    for k in range(2):
        high, low = split(sens_ref[0, k])
        picked = dot(row_bus, high, NN) + dot(row_bus, low, NN)
        high, low = split(picked)
        parts.append(dot(high, column_bus, NT) + dot(low, column_bus, NT))
    return jnp.concatenate(
        [parts[k][s * blocks : (s + 1) * blocks] for s in range(CAP) for k in range(2)], 1
    )


def drives_of(group, load_ref, map_ref):
    per_dev, span, scen, nodes = load_ref.shape
    return [dot(load_ref[f].reshape(span * scen, nodes), map_ref[f], NN) for f in group]


def states_of(f, drive, decay_ref):
    span = decay_ref.shape[0]
    scen = drive.shape[0] // span
    state = drive[:scen]
    states = [state]
    for t in range(1, span):
        state = decay_ref[t, f : f + 1, :] * state + drive[t * scen : (t + 1) * scen]
        states.append(state)
    return states


def started(pairs, sems):
    copies = [
        pltpu.make_async_copy(source, target, sems.at[i])
        for i, (source, target) in enumerate(pairs)
    ]
    for copy in copies:
        copy.start()
    return copies


def started_feeders(load_hbm, load_ref, load_sems, map_hbm, map_ref, map_sems):
    per_dev = load_ref.shape[0]
    loads = [
        pltpu.make_async_copy(load_hbm.at[f], load_ref.at[f], load_sems.at[f])
        for f in range(per_dev)
    ]
    maps = [
        pltpu.make_async_copy(map_hbm.at[f], map_ref.at[f], map_sems.at[f])
        for f in range(per_dev)
    ]
    for f in range(per_dev):
        loads[f].start(priority=1)
        maps[f].start(priority=0)
    return loads, maps


def groups_of(sizes):
    groups, begin = [], 0
    for size in sizes:
        groups.append(range(begin, begin + size))
        begin += size
    return groups


def drive_kernel(
    counts_hbm, load_hbm, map_hbm, decay_hbm,
    send_hbm,
    send_ref, counts_ref, load_ref, map_ref, decay_ref,
    load_sems, map_sems, send_sems, sems,
):
    per_dev, span, scen, nodes = load_ref.shape
    width = map_ref.shape[2]
    small = started([(counts_hbm, counts_ref), (decay_hbm, decay_ref)], sems)
    loads, maps = started_feeders(load_hbm, load_ref, load_sems, map_hbm, map_ref, map_sems)
    for copy in small:
        copy.wait()
    blank = jnp.zeros((send_ref.shape[1] - scen - span, width), F32)
    sends = [
        pltpu.make_async_copy(send_ref.at[f], send_hbm.at[f], send_sems.at[f])
        for f in range(per_dev)
    ]
    state_id = lax.broadcasted_iota(jnp.int32, (1, width), 1)
    for group in groups_of(GROUPS):
        for f in group:
            maps[f].wait()
            loads[f].wait()
        drives = drives_of(group, load_ref, map_ref)
        for f, drive in zip(group, drives):
            send_ref[f, 0:scen] = jnp.where(
                state_id < counts_ref[f], states_of(f, drive, decay_ref)[-1], 0.0
            )
            send_ref[f, scen:] = jnp.concatenate(
                [decay_ref[t, f : f + 1, :] for t in range(span)] + [blank], 0
            )
        for f in group:
            sends[f].start()
    for copy in sends:
        copy.wait()


def side_kernel(
    counts_hbm, load_hbm, map_hbm, decay_hbm, out_hbm, area_ref, bus_ref, rule_ref, sens_hbm,
    knots_ref, levels_ref,
    flow_ref, table_ref,
    counts_ref, load_ref, map_ref, decay_ref, out_ref, sens_ref,
    load_sems, map_sems, sems,
):
    per_dev, span, scen, nodes = load_ref.shape
    lanes = flow_ref.shape[2]
    small = started(
        [
            (counts_hbm, counts_ref),
            (decay_hbm, decay_ref),
            (out_hbm, out_ref),
            (sens_hbm, sens_ref),
        ],
        sems,
    )
    loads, maps = started_feeders(load_hbm, load_ref, load_sems, map_hbm, map_ref, map_sems)
    areas = area_ref[...]
    rules = rule_ref[...]
    count = areas.shape[1]
    blocks = count // per_dev
    members = blocks * CAP
    slots, ranks = member_slots(areas, per_dev)
    me = lax.axis_index("feeder")
    feeder = lax.broadcasted_iota(jnp.int32, (per_dev, count), 1)
    here = feeder == me * per_dev + lax.broadcasted_iota(jnp.int32, (per_dev, count), 0)
    my_area = jnp.sum(jnp.where(here, areas, 0), axis=1, keepdims=True)
    my_rank = jnp.sum(jnp.where(here, ranks, 0), axis=1, keepdims=True)
    my_rule = jnp.sum(jnp.where(here, rules, 0), axis=1, keepdims=True)
    choice = lax.broadcasted_iota(jnp.int32, (per_dev, blocks), 1)
    hot = (choice == my_area).astype(F32)
    own = (areas == my_area).astype(F32)
    lane = lax.broadcasted_iota(jnp.int32, (per_dev, lanes), 1)
    of_rank = lax.div(lane, lanes // CAP) == my_rank
    of_k = lax.rem(lax.div(lane, members), 2)
    masks = [(of_rank & (of_k == k)).astype(F32) for k in range(2)]
    rule_count = knots_ref.shape[1]
    rule_choice = lax.broadcasted_iota(jnp.int32, (per_dev, rule_count), 1)
    rule_hot = (rule_choice == my_rule).astype(BF16)
    knots = knots_ref.shape[0]

    def looked_up(table_ref):
        high, low = split(table_ref[...].astype(F32))
        return (dot(rule_hot, high, NT) + dot(rule_hot, low, NT)) / 1000.0

    knot_volts = looked_up(knots_ref)
    knot_levels = looked_up(levels_ref)
    width = knot_volts[:, 1:] - knot_volts[:, : knots - 1]
    slope = (knot_levels[:, 1:] - knot_levels[:, : knots - 1]) / width
    table_ref[OWN, :, :] = own
    for k in range(2):
        table_ref[MASKS, :, k * lanes : (k + 1) * lanes] = masks[k]
    table_ref[HOT, :, :blocks] = hot
    table_ref[SLOT, :, :] = slots.astype(F32) + jnp.zeros((per_dev, count), F32)
    table_ref[KNOT, :, :knots] = knot_volts
    table_ref[KNOT, :, lanes : lanes + 1] = knot_levels[:, 0:1]
    table_ref[SLOPE, :, : knots - 1] = width
    table_ref[SLOPE, :, lanes : lanes + knots - 1] = slope
    for copy in small:
        copy.wait()
    planes = flow_ref.shape[0] - 1
    flow_ref[planes] = area_matrix(areas, slots, bus_ref[...], sens_ref, per_dev)
    state_id = lax.broadcasted_iota(jnp.int32, (1, map_ref.shape[2]), 1)
    for group in groups_of(GROUPS):
        for f in group:
            maps[f].wait()
            loads[f].wait()
        drives = drives_of(group, load_ref, map_ref)
        histories = [states_of(f, drive, decay_ref) for f, drive in zip(group, drives)]
        for f, history in zip(group, histories):
            out = jnp.where(state_id < counts_ref[f], out_ref[f], 0.0)
            flow = dot3(out, jnp.concatenate(history, 0), NT)
            for k in range(2):
                for piece in range(planes // 2):
                    flow_ref[k * (planes // 2) + piece, f : f + 1, :] = flow[
                        k : k + 1, piece * lanes : (piece + 1) * lanes
                    ]


def owner_kernel(recv_ref, out_ref, back_ref):
    chunks, rows, width = recv_ref.shape
    scen = back_ref.shape[2] // 2
    span = 6
    me = lax.axis_index("tm")
    out = out_ref[me]
    state = recv_ref[0, 0:scen]
    back_ref[0] = jnp.zeros(back_ref.shape[1:], F32)
    for chunk in range(1, chunks):
        product = recv_ref[chunk, scen : scen + 1]
        kept = [product]
        for t in range(1, span):
            product = product * recv_ref[chunk, scen + t : scen + t + 1]
            kept.append(product)
        blank = jnp.zeros((2, width), F32)
        even = [out[k : k + 1] * kept[t] for k in range(2) for t in range(0, span, 2)]
        odd = [out[k : k + 1] * kept[t] for k in range(2) for t in range(1, span, 2)]
        weights = jnp.concatenate(even + [blank] + odd + [blank], 0)
        flow = dot3(weights, state, NT)
        back_ref[chunk] = jnp.concatenate([flow[:8], flow[8:]], 1)
        if chunk < chunks - 1:
            state = recv_ref[chunk, 0:scen] + product * state


def join_kernel(back_ref, flow_ref, all_ref):
    planes = flow_ref.shape[0] - 1
    for plane in range(planes):
        all_ref[plane] = flow_ref[plane] + back_ref[:, plane, :]
    all_ref[planes] = flow_ref[planes]


def mix_kernel(knots, table_ref, every_ref, result_ref):
    blocks, planes, per_dev, lanes = every_ref.shape
    planes = planes - 1
    count = blocks * per_dev
    members = blocks * CAP
    me = lax.axis_index("feeder")
    hot = table_ref[HOT, :, :blocks].astype(BF16)
    masks = [
        table_ref[MASKS, :, k * lanes : (k + 1) * lanes].astype(BF16) for k in range(2)
    ]
    row = lax.rem(lax.broadcasted_iota(jnp.int32, (lanes, count), 0), members)
    spread = (row.astype(F32) == table_ref[SLOT, 0:1, :]).astype(BF16)
    high, low = split(every_ref[:, planes, pl.ds(me, 1), :].reshape(blocks, lanes))
    weight = jnp.zeros((2 * per_dev, count), F32)
    for part in (high, low):
        picked = dot(hot, part, NN).astype(BF16)
        weight = weight + dot(
            jnp.concatenate([picked * masks[0], picked * masks[1]], 0), spread, NN
        )
    own = table_ref[OWN]
    weights = [weight[k * per_dev : (k + 1) * per_dev] * own for k in range(2)]
    per_k = planes // 2
    scen = result_ref.shape[2]
    knot_volts = table_ref[KNOT, :, :knots]
    first = table_ref[KNOT, :, lanes : lanes + 1]
    widths = table_ref[SLOPE, :, : knots - 1]
    slopes = table_ref[SLOPE, :, lanes : lanes + knots - 1]
    for piece in range(per_k):
        volts = sum(
            dot3(weights[k], every_ref[:, k * per_k + piece].reshape(count, lanes), NN)
            for k in range(2)
        )
        result = first + jnp.zeros_like(volts)
        for j in range(knots - 1):
            result = result + slopes[:, j : j + 1] * jnp.minimum(
                jnp.maximum(volts - knot_volts[:, j : j + 1], 0.0), widths[:, j : j + 1]
            )
        result_ref[2 * piece] = result[:, :scen]
        result_ref[2 * piece + 1] = result[:, scen:]


def drive_call(counts, load, drive_map, decay):
    per_dev, span, scen, _ = load.shape
    width = drive_map.shape[2]
    rows = scen + 8
    operands = (load, drive_map, decay)
    return pl.pallas_call(
        drive_kernel,
        in_specs=[ANYWHERE] * 4,
        out_specs=ANYWHERE,
        out_shape=jax.ShapeDtypeStruct((per_dev, rows, width), F32),
        scratch_shapes=[
            pltpu.VMEM((per_dev, rows, width), F32),
            pltpu.SMEM(counts.shape, counts.dtype),
        ]
        + [pltpu.VMEM(x.shape, x.dtype) for x in operands]
        + [pltpu.SemaphoreType.DMA((per_dev,))] * 3
        + [pltpu.SemaphoreType.DMA((2,))],
        compiler_params=pltpu.CompilerParams(vmem_limit_bytes=58 * 1024 * 1024),
        name="drive",
    )(counts, *operands)


def side_call(
    counts, load, drive_map, decay, out_map, area_row, bus_row, rule_row, sensitivity,
    knots, levels,
):
    per_dev, span, scen, nodes = load.shape
    width = drive_map.shape[2]
    lanes = 2 * scen
    count = area_row.shape[1]
    shapes = [(span + 1, per_dev, lanes), (6, per_dev, count)]
    copied = (load, drive_map, decay, out_map, sensitivity)
    return pl.pallas_call(
        side_kernel,
        in_specs=[ANYWHERE] * 5 + [WHOLE] * 3 + [ANYWHERE] + [WHOLE] * 2,
        out_specs=[WHOLE] * len(shapes),
        out_shape=[pltpu.VMEM(shape, F32) for shape in shapes],
        scratch_shapes=[pltpu.SMEM(counts.shape, counts.dtype)]
        + [pltpu.VMEM(x.shape, x.dtype) for x in copied]
        + [pltpu.SemaphoreType.DMA((per_dev,))] * 2
        + [pltpu.SemaphoreType.DMA((4,))],
        compiler_params=pltpu.CompilerParams(vmem_limit_bytes=56 * 1024 * 1024),
        cost_estimate=pl.CostEstimate(
            flops=2 * per_dev * span * scen * nodes * width,
            bytes_accessed=20 * 1024 * 1024,
            transcendentals=0,
        ),
        name="side",
    )(
        counts, load, drive_map, decay, out_map, area_row, bus_row, rule_row, sensitivity,
        knots, levels,
    )


def per_device(
    node_load, drive_map, decay_rate, counts, out_map, area_of, head_bus, rule_of,
    rule_knots, levels, sensitivity,
):
    per_dev, scen, span, nodes = node_load.shape
    feeders = area_of.shape[0]
    chunks = lax.axis_size("tm")
    lanes = 2 * scen
    load = jnp.transpose(node_load, (0, 2, 1, 3))
    decay = jnp.transpose(decay_rate, (1, 0, 2))

    send = drive_call(counts, load, drive_map, decay)
    owned = lax.all_to_all(send, "tm", 0, 0, tiled=True)
    flow, table = side_call(
        counts, load, drive_map, decay, out_map,
        jnp.transpose(area_of, (1, 0)), head_bus.reshape(1, feeders),
        rule_of.reshape(1, feeders), sensitivity,
        jnp.transpose(rule_knots, (1, 0)), jnp.transpose(levels, (1, 0)),
    )
    owned, flow, table = lax.optimization_barrier((owned, flow, table))
    back = pl.pallas_call(
        owner_kernel,
        in_specs=[WHOLE, WHOLE],
        out_specs=WHOLE,
        out_shape=pltpu.VMEM((chunks, 8, lanes), F32),
        compiler_params=pltpu.CompilerParams(vmem_limit_bytes=16 * 1024 * 1024),
        name="owner",
    )(owned, out_map)
    back = lax.all_to_all(back, "tm", 0, 0, tiled=True)
    joined = pl.pallas_call(
        join_kernel,
        in_specs=[WHOLE] * 2,
        out_specs=WHOLE,
        out_shape=pltpu.VMEM(flow.shape, F32),
        compiler_params=pltpu.CompilerParams(vmem_limit_bytes=8 * 1024 * 1024),
        name="join",
    )(back, flow)
    every = lax.all_gather(joined, "feeder", axis=0, tiled=False)
    result = pl.pallas_call(
        functools.partial(mix_kernel, levels.shape[1]),
        in_specs=[WHOLE] * 2,
        out_specs=WHOLE,
        out_shape=jax.ShapeDtypeStruct((span, per_dev, scen), F32),
        compiler_params=pltpu.CompilerParams(vmem_limit_bytes=16 * 1024 * 1024),
        name="mix",
    )(table, every)
    return jnp.transpose(result, (1, 0, 2))


def solution(mesh):
    return jax.shard_map(
        per_device,
        mesh=mesh,
        in_specs=(
            P("feeder", None, "tm", None),
            P("feeder", None, None),
            P("feeder", "tm", None),
            P("feeder"),
            P("feeder", None, None),
            P(),
            P(),
            P(),
            P(),
            P(),
            P("feeder", None, None, None),
        ),
        out_specs=P("feeder", "tm", None),
        check_vma=False,
    )
```

```python
import functools

import jax
import jax.numpy as jnp
from jax import lax
from jax.experimental import pallas as pl
from jax.experimental.pallas import tpu as pltpu
from jax.sharding import PartitionSpec as P

F32 = jnp.float32
BF16 = jnp.bfloat16
CAP = 2
OWN, MASKS, HOT, SLOT, KNOT, SLOPE = range(6)
GROUPS = (6, 6, 4)
NT = (((1,), (1,)), ((), ()))
NN = (((1,), (0,)), ((), ()))
WHOLE = pl.BlockSpec(memory_space=pltpu.VMEM)
ANYWHERE = pl.BlockSpec(memory_space=pl.ANY)


def split(x):
    high = x.astype(BF16)
    return high, (x - high.astype(F32)).astype(BF16)


def dot(a, b, dims):
    return lax.dot_general(a, b, dims, preferred_element_type=F32)


def dot3(a, b, dims):
    a_high, a_low = split(a)
    b_high, b_low = split(b)
    rows = a.shape[0]
    both = dot(jnp.concatenate([a_high, a_low], 0), b_high, dims)
    return both[:rows] + both[rows:] + dot(a_high, b_low, dims)


def member_slots(areas, block):
    lane = lax.broadcasted_iota(jnp.int32, areas.shape, 1)
    within = lax.rem(lane, block)
    rank = jnp.zeros_like(areas)
    for back in range(1, block):
        same = (areas == pltpu.roll(areas, back, 1)) & (within >= back)
        rank = rank + same.astype(jnp.int32)
    return lax.div(lane, block) * CAP + rank, rank


def area_matrix(areas, slots, buses, sens_ref, per_dev):
    count = areas.shape[1]
    bus_count = sens_ref.shape[2]
    blocks = count // per_dev
    members = blocks * CAP
    mine = areas == lax.axis_index("feeder")
    bus_hot = (lax.broadcasted_iota(jnp.int32, (bus_count, count), 0) == buses).astype(BF16)
    row = lax.broadcasted_iota(jnp.int32, (members, count), 0)
    wanted = jnp.where(row < blocks, row * CAP, (row - blocks) * CAP + 1)
    by_rank = ((wanted == slots) & mine).astype(BF16)
    by_slot = ((row == slots) & mine).astype(BF16)
    row_bus = dot(by_rank, bus_hot, NT).astype(BF16)
    column_bus = dot(by_slot, bus_hot, NT).astype(BF16)
    parts = []
    for k in range(2):
        high, low = split(sens_ref[0, k])
        picked = dot(row_bus, high, NN) + dot(row_bus, low, NN)
        high, low = split(picked)
        parts.append(dot(high, column_bus, NT) + dot(low, column_bus, NT))
    return jnp.concatenate(
        [parts[k][s * blocks : (s + 1) * blocks] for s in range(CAP) for k in range(2)], 1
    )


def drives_of(group, load_ref, map_ref):
    per_dev, span, scen, nodes = load_ref.shape
    return [dot(load_ref[f].reshape(span * scen, nodes), map_ref[f], NN) for f in group]


def states_of(f, drive, decay_ref):
    span = decay_ref.shape[0]
    scen = drive.shape[0] // span
    state = drive[:scen]
    states = [state]
    for t in range(1, span):
        state = decay_ref[t, f : f + 1, :] * state + drive[t * scen : (t + 1) * scen]
        states.append(state)
    return states


def started(pairs, sems):
    copies = [
        pltpu.make_async_copy(source, target, sems.at[i])
        for i, (source, target) in enumerate(pairs)
    ]
    for copy in copies:
        copy.start()
    return copies


def started_feeders(load_hbm, load_ref, load_sems, map_hbm, map_ref, map_sems):
    per_dev = load_ref.shape[0]
    loads = [
        pltpu.make_async_copy(load_hbm.at[f], load_ref.at[f], load_sems.at[f])
        for f in range(per_dev)
    ]
    maps = [
        pltpu.make_async_copy(map_hbm.at[f], map_ref.at[f], map_sems.at[f])
        for f in range(per_dev)
    ]
    for f in range(per_dev):
        loads[f].start(priority=1)
        maps[f].start(priority=0)
    return loads, maps


def groups_of(sizes):
    groups, begin = [], 0
    for size in sizes:
        groups.append(range(begin, begin + size))
        begin += size
    return groups


def drive_kernel(
    counts_hbm, load_hbm, map_hbm, decay_hbm,
    send_hbm,
    send_ref, counts_ref, load_ref, map_ref, decay_ref,
    load_sems, map_sems, send_sems, sems,
):
    per_dev, span, scen, nodes = load_ref.shape
    width = map_ref.shape[2]
    small = started([(counts_hbm, counts_ref), (decay_hbm, decay_ref)], sems)
    loads, maps = started_feeders(load_hbm, load_ref, load_sems, map_hbm, map_ref, map_sems)
    for copy in small:
        copy.wait()
    sends = [
        pltpu.make_async_copy(send_ref.at[f], send_hbm.at[f], send_sems.at[f])
        for f in range(per_dev)
    ]
    state_id = lax.broadcasted_iota(jnp.int32, (1, width), 1)
    for group in groups_of(GROUPS):
        for f in group:
            maps[f].wait()
            loads[f].wait()
        drives = drives_of(group, load_ref, map_ref)
        for f, drive in zip(group, drives):
            send_ref[f, 0:scen] = jnp.where(
                state_id < counts_ref[f], states_of(f, drive, decay_ref)[-1], 0.0
            )
            send_ref[f, scen:] = jnp.concatenate(
                [decay_ref[t, f : f + 1, :] for t in range(span)], 0
            )
        for f in group:
            sends[f].start()
    for copy in sends:
        copy.wait()


def side_kernel(
    counts_hbm, load_hbm, map_hbm, decay_hbm, out_hbm, area_ref, bus_ref, rule_ref, sens_hbm,
    knots_ref, levels_ref,
    flow_ref, table_ref,
    counts_ref, load_ref, map_ref, decay_ref, out_ref, sens_ref,
    load_sems, map_sems, sems,
):
    per_dev, span, scen, nodes = load_ref.shape
    lanes = flow_ref.shape[2]
    small = started(
        [
            (counts_hbm, counts_ref),
            (decay_hbm, decay_ref),
            (out_hbm, out_ref),
            (sens_hbm, sens_ref),
        ],
        sems,
    )
    loads, maps = started_feeders(load_hbm, load_ref, load_sems, map_hbm, map_ref, map_sems)
    areas = area_ref[...]
    rules = rule_ref[...]
    count = areas.shape[1]
    blocks = count // per_dev
    members = blocks * CAP
    slots, ranks = member_slots(areas, per_dev)
    me = lax.axis_index("feeder")
    feeder = lax.broadcasted_iota(jnp.int32, (per_dev, count), 1)
    here = feeder == me * per_dev + lax.broadcasted_iota(jnp.int32, (per_dev, count), 0)
    my_area = jnp.sum(jnp.where(here, areas, 0), axis=1, keepdims=True)
    my_rank = jnp.sum(jnp.where(here, ranks, 0), axis=1, keepdims=True)
    my_rule = jnp.sum(jnp.where(here, rules, 0), axis=1, keepdims=True)
    choice = lax.broadcasted_iota(jnp.int32, (per_dev, blocks), 1)
    hot = (choice == my_area).astype(F32)
    own = (areas == my_area).astype(F32)
    lane = lax.broadcasted_iota(jnp.int32, (per_dev, lanes), 1)
    of_rank = lax.div(lane, lanes // CAP) == my_rank
    of_k = lax.rem(lax.div(lane, members), 2)
    masks = [(of_rank & (of_k == k)).astype(F32) for k in range(2)]
    rule_count = knots_ref.shape[1]
    rule_choice = lax.broadcasted_iota(jnp.int32, (per_dev, rule_count), 1)
    rule_hot = (rule_choice == my_rule).astype(BF16)
    knots = knots_ref.shape[0]

    def looked_up(table_ref):
        high, low = split(table_ref[...].astype(F32))
        return (dot(rule_hot, high, NT) + dot(rule_hot, low, NT)) / 1000.0

    knot_volts = looked_up(knots_ref)
    knot_levels = looked_up(levels_ref)
    width = knot_volts[:, 1:] - knot_volts[:, : knots - 1]
    slope = (knot_levels[:, 1:] - knot_levels[:, : knots - 1]) / width
    table_ref[OWN, :, :] = own
    for k in range(2):
        table_ref[MASKS, :, k * lanes : (k + 1) * lanes] = masks[k]
    table_ref[HOT, :, :blocks] = hot
    table_ref[SLOT, :, :] = slots.astype(F32) + jnp.zeros((per_dev, count), F32)
    table_ref[KNOT, :, :knots] = knot_volts
    table_ref[KNOT, :, lanes : lanes + 1] = knot_levels[:, 0:1]
    table_ref[SLOPE, :, : knots - 1] = width
    table_ref[SLOPE, :, lanes : lanes + knots - 1] = slope
    for copy in small:
        copy.wait()
    planes = flow_ref.shape[0] - 1
    flow_ref[planes] = area_matrix(areas, slots, bus_ref[...], sens_ref, per_dev)
    state_id = lax.broadcasted_iota(jnp.int32, (1, map_ref.shape[2]), 1)
    for group in groups_of(GROUPS):
        for f in group:
            maps[f].wait()
            loads[f].wait()
        drives = drives_of(group, load_ref, map_ref)
        histories = [states_of(f, drive, decay_ref) for f, drive in zip(group, drives)]
        for f, history in zip(group, histories):
            out = jnp.where(state_id < counts_ref[f], out_ref[f], 0.0)
            flow = dot3(out, jnp.concatenate(history, 0), NT)
            for k in range(2):
                for piece in range(planes // 2):
                    flow_ref[k * (planes // 2) + piece, f : f + 1, :] = flow[
                        k : k + 1, piece * lanes : (piece + 1) * lanes
                    ]


def owner_kernel(recv_ref, out_ref, back_ref):
    chunks, rows, width = recv_ref.shape
    scen = back_ref.shape[2] // 2
    span = 6
    me = lax.axis_index("tm")
    out = out_ref[me]
    state = recv_ref[0, 0:scen]
    back_ref[0] = jnp.zeros(back_ref.shape[1:], F32)
    for chunk in range(1, chunks):
        product = recv_ref[chunk, scen : scen + 1]
        kept = [product]
        for t in range(1, span):
            product = product * recv_ref[chunk, scen + t : scen + t + 1]
            kept.append(product)
        blank = jnp.zeros((2, width), F32)
        even = [out[k : k + 1] * kept[t] for k in range(2) for t in range(0, span, 2)]
        odd = [out[k : k + 1] * kept[t] for k in range(2) for t in range(1, span, 2)]
        weights = jnp.concatenate(even + [blank] + odd + [blank], 0)
        flow = dot3(weights, state, NT)
        back_ref[chunk] = jnp.concatenate([flow[:8], flow[8:]], 1)
        if chunk < chunks - 1:
            state = recv_ref[chunk, 0:scen] + product * state


def join_kernel(back_ref, flow_ref, all_ref):
    planes = flow_ref.shape[0] - 1
    for plane in range(planes):
        all_ref[plane] = flow_ref[plane] + back_ref[:, plane, :]
    all_ref[planes] = flow_ref[planes]


def mix_kernel(knots, table_ref, every_ref, result_ref):
    blocks, planes, per_dev, lanes = every_ref.shape
    planes = planes - 1
    count = blocks * per_dev
    members = blocks * CAP
    me = lax.axis_index("feeder")
    hot = table_ref[HOT, :, :blocks].astype(BF16)
    masks = [
        table_ref[MASKS, :, k * lanes : (k + 1) * lanes].astype(BF16) for k in range(2)
    ]
    row = lax.rem(lax.broadcasted_iota(jnp.int32, (lanes, count), 0), members)
    spread = (row.astype(F32) == table_ref[SLOT, 0:1, :]).astype(BF16)
    high, low = split(every_ref[:, planes, pl.ds(me, 1), :].reshape(blocks, lanes))
    weight = jnp.zeros((2 * per_dev, count), F32)
    for part in (high, low):
        picked = dot(hot, part, NN).astype(BF16)
        weight = weight + dot(
            jnp.concatenate([picked * masks[0], picked * masks[1]], 0), spread, NN
        )
    own = table_ref[OWN]
    weights = [weight[k * per_dev : (k + 1) * per_dev] * own for k in range(2)]
    per_k = planes // 2
    scen = result_ref.shape[2]
    knot_volts = table_ref[KNOT, :, :knots]
    first = table_ref[KNOT, :, lanes : lanes + 1]
    widths = table_ref[SLOPE, :, : knots - 1]
    slopes = table_ref[SLOPE, :, lanes : lanes + knots - 1]
    for piece in range(per_k):
        volts = sum(
            dot3(weights[k], every_ref[:, k * per_k + piece].reshape(count, lanes), NN)
            for k in range(2)
        )
        result = first + jnp.zeros_like(volts)
        for j in range(knots - 1):
            result = result + slopes[:, j : j + 1] * jnp.minimum(
                jnp.maximum(volts - knot_volts[:, j : j + 1], 0.0), widths[:, j : j + 1]
            )
        result_ref[2 * piece] = result[:, :scen]
        result_ref[2 * piece + 1] = result[:, scen:]


def drive_call(counts, load, drive_map, decay):
    per_dev, span, scen, _ = load.shape
    width = drive_map.shape[2]
    rows = scen + span
    operands = (load, drive_map, decay)
    return pl.pallas_call(
        drive_kernel,
        in_specs=[ANYWHERE] * 4,
        out_specs=ANYWHERE,
        out_shape=jax.ShapeDtypeStruct((per_dev, rows, width), F32),
        scratch_shapes=[
            pltpu.VMEM((per_dev, rows, width), F32),
            pltpu.SMEM(counts.shape, counts.dtype),
        ]
        + [pltpu.VMEM(x.shape, x.dtype) for x in operands]
        + [pltpu.SemaphoreType.DMA((per_dev,))] * 3
        + [pltpu.SemaphoreType.DMA((2,))],
        compiler_params=pltpu.CompilerParams(vmem_limit_bytes=58 * 1024 * 1024),
        name="drive",
    )(counts, *operands)


def side_call(
    counts, load, drive_map, decay, out_map, area_row, bus_row, rule_row, sensitivity,
    knots, levels,
):
    per_dev, span, scen, nodes = load.shape
    width = drive_map.shape[2]
    lanes = 2 * scen
    count = area_row.shape[1]
    shapes = [(span + 1, per_dev, lanes), (6, per_dev, count)]
    copied = (load, drive_map, decay, out_map, sensitivity)
    return pl.pallas_call(
        side_kernel,
        in_specs=[ANYWHERE] * 5 + [WHOLE] * 3 + [ANYWHERE] + [WHOLE] * 2,
        out_specs=[WHOLE] * len(shapes),
        out_shape=[pltpu.VMEM(shape, F32) for shape in shapes],
        scratch_shapes=[pltpu.SMEM(counts.shape, counts.dtype)]
        + [pltpu.VMEM(x.shape, x.dtype) for x in copied]
        + [pltpu.SemaphoreType.DMA((per_dev,))] * 2
        + [pltpu.SemaphoreType.DMA((4,))],
        compiler_params=pltpu.CompilerParams(vmem_limit_bytes=56 * 1024 * 1024),
        cost_estimate=pl.CostEstimate(
            flops=2 * per_dev * span * scen * nodes * width,
            bytes_accessed=20 * 1024 * 1024,
            transcendentals=0,
        ),
        name="side",
    )(
        counts, load, drive_map, decay, out_map, area_row, bus_row, rule_row, sensitivity,
        knots, levels,
    )


def per_device(
    node_load, drive_map, decay_rate, counts, out_map, area_of, head_bus, rule_of,
    rule_knots, levels, sensitivity,
):
    per_dev, scen, span, nodes = node_load.shape
    feeders = area_of.shape[0]
    chunks = lax.axis_size("tm")
    lanes = 2 * scen
    load = jnp.transpose(node_load, (0, 2, 1, 3))
    decay = jnp.transpose(decay_rate, (1, 0, 2))

    send = drive_call(counts, load, drive_map, decay)
    owned = lax.all_to_all(send, "tm", 0, 0, tiled=True)
    flow, table = side_call(
        counts, load, drive_map, decay, out_map,
        jnp.transpose(area_of, (1, 0)), head_bus.reshape(1, feeders),
        rule_of.reshape(1, feeders), sensitivity,
        jnp.transpose(rule_knots, (1, 0)), jnp.transpose(levels, (1, 0)),
    )
    owned, flow, table = lax.optimization_barrier((owned, flow, table))
    back = pl.pallas_call(
        owner_kernel,
        in_specs=[WHOLE, WHOLE],
        out_specs=WHOLE,
        out_shape=pltpu.VMEM((chunks, 8, lanes), F32),
        compiler_params=pltpu.CompilerParams(vmem_limit_bytes=16 * 1024 * 1024),
        name="owner",
    )(owned, out_map)
    back = lax.all_to_all(back, "tm", 0, 0, tiled=True)
    joined = pl.pallas_call(
        join_kernel,
        in_specs=[WHOLE] * 2,
        out_specs=WHOLE,
        out_shape=pltpu.VMEM(flow.shape, F32),
        compiler_params=pltpu.CompilerParams(vmem_limit_bytes=8 * 1024 * 1024),
        name="join",
    )(back, flow)
    every = lax.all_gather(joined, "feeder", axis=0, tiled=False)
    result = pl.pallas_call(
        functools.partial(mix_kernel, levels.shape[1]),
        in_specs=[WHOLE] * 2,
        out_specs=WHOLE,
        out_shape=jax.ShapeDtypeStruct((span, per_dev, scen), F32),
        compiler_params=pltpu.CompilerParams(vmem_limit_bytes=16 * 1024 * 1024),
        name="mix",
    )(table, every)
    return jnp.transpose(result, (1, 0, 2))


def solution(mesh):
    return jax.shard_map(
        per_device,
        mesh=mesh,
        in_specs=(
            P("feeder", None, "tm", None),
            P("feeder", None, None),
            P("feeder", "tm", None),
            P("feeder"),
            P("feeder", None, None),
            P(),
            P(),
            P(),
            P(),
            P(),
            P("feeder", None, None, None),
        ),
        out_specs=P("feeder", "tm", None),
        check_vma=False,
    )
```

```python
import functools

import jax
import jax.numpy as jnp
from jax import lax
from jax.experimental import pallas as pl
from jax.experimental.pallas import tpu as pltpu
from jax.sharding import PartitionSpec as P

F32 = jnp.float32
BF16 = jnp.bfloat16
CAP = 2
OWN, MASKS, HOT, SLOT, KNOT, SLOPE = range(6)
GROUPS = (6, 6, 4)
NT = (((1,), (1,)), ((), ()))
NN = (((1,), (0,)), ((), ()))
WHOLE = pl.BlockSpec(memory_space=pltpu.VMEM)
ANYWHERE = pl.BlockSpec(memory_space=pl.ANY)


def split(x):
    high = x.astype(BF16)
    return high, (x - high.astype(F32)).astype(BF16)


def dot(a, b, dims):
    return lax.dot_general(a, b, dims, preferred_element_type=F32)


def dot3(a, b, dims):
    a_high, a_low = split(a)
    b_high, b_low = split(b)
    rows = a.shape[0]
    both = dot(jnp.concatenate([a_high, a_low], 0), b_high, dims)
    return both[:rows] + both[rows:] + dot(a_high, b_low, dims)


def member_slots(areas, block):
    lane = lax.broadcasted_iota(jnp.int32, areas.shape, 1)
    within = lax.rem(lane, block)
    rank = jnp.zeros_like(areas)
    for back in range(1, block):
        same = (areas == pltpu.roll(areas, back, 1)) & (within >= back)
        rank = rank + same.astype(jnp.int32)
    return lax.div(lane, block) * CAP + rank, rank


def area_matrix(areas, slots, buses, sens_ref, per_dev):
    count = areas.shape[1]
    bus_count = sens_ref.shape[2]
    blocks = count // per_dev
    members = blocks * CAP
    mine = areas == lax.axis_index("feeder")
    bus_hot = (lax.broadcasted_iota(jnp.int32, (bus_count, count), 0) == buses).astype(BF16)
    row = lax.broadcasted_iota(jnp.int32, (members, count), 0)
    wanted = jnp.where(row < blocks, row * CAP, (row - blocks) * CAP + 1)
    by_rank = ((wanted == slots) & mine).astype(BF16)
    by_slot = ((row == slots) & mine).astype(BF16)
    row_bus = dot(by_rank, bus_hot, NT).astype(BF16)
    column_bus = dot(by_slot, bus_hot, NT).astype(BF16)
    parts = []
    for k in range(2):
        high, low = split(sens_ref[0, k])
        picked = dot(row_bus, high, NN) + dot(row_bus, low, NN)
        high, low = split(picked)
        parts.append(dot(high, column_bus, NT) + dot(low, column_bus, NT))
    return jnp.concatenate(
        [parts[k][s * blocks : (s + 1) * blocks] for s in range(CAP) for k in range(2)], 1
    )


def drives_of(group, load_ref, map_ref):
    per_dev, span, scen, nodes = load_ref.shape
    return [dot(load_ref[f].reshape(span * scen, nodes), map_ref[f], NN) for f in group]


def states_of(f, drive, decay_ref):
    span = decay_ref.shape[0]
    scen = drive.shape[0] // span
    state = drive[:scen]
    states = [state]
    for t in range(1, span):
        state = decay_ref[t, f : f + 1, :] * state + drive[t * scen : (t + 1) * scen]
        states.append(state)
    return states


def started(pairs, sems):
    copies = [
        pltpu.make_async_copy(source, target, sems.at[i])
        for i, (source, target) in enumerate(pairs)
    ]
    for copy in copies:
        copy.start()
    return copies


def started_feeders(load_hbm, load_ref, load_sems, map_hbm, map_ref, map_sems):
    per_dev = load_ref.shape[0]
    loads = [
        pltpu.make_async_copy(load_hbm.at[f], load_ref.at[f], load_sems.at[f])
        for f in range(per_dev)
    ]
    maps = [
        pltpu.make_async_copy(map_hbm.at[f], map_ref.at[f], map_sems.at[f])
        for f in range(per_dev)
    ]
    for f in range(per_dev):
        loads[f].start(priority=1)
        maps[f].start(priority=0)
    return loads, maps


def groups_of(sizes):
    groups, begin = [], 0
    for size in sizes:
        groups.append(range(begin, begin + size))
        begin += size
    return groups


def drive_kernel(
    counts_hbm, load_hbm, map_hbm, decay_hbm,
    send_hbm,
    send_ref, counts_ref, load_ref, map_ref, decay_ref,
    load_sems, map_sems, send_sems, sems,
):
    per_dev, span, scen, nodes = load_ref.shape
    width = map_ref.shape[2]
    small = started([(counts_hbm, counts_ref), (decay_hbm, decay_ref)], sems)
    loads, maps = started_feeders(load_hbm, load_ref, load_sems, map_hbm, map_ref, map_sems)
    for copy in small:
        copy.wait()
    sends = [
        pltpu.make_async_copy(send_ref.at[f], send_hbm.at[f], send_sems.at[f])
        for f in range(per_dev)
    ]
    state_id = lax.broadcasted_iota(jnp.int32, (1, width), 1)
    for group in groups_of(GROUPS):
        for f in group:
            maps[f].wait()
            loads[f].wait()
        drives = drives_of(group, load_ref, map_ref)
        for f, drive in zip(group, drives):
            send_ref[f, 0:scen] = jnp.where(
                state_id < counts_ref[f], states_of(f, drive, decay_ref)[-1], 0.0
            )
            send_ref[f, scen:] = jnp.concatenate(
                [decay_ref[t, f : f + 1, :] for t in range(span)], 0
            )
        for f in group:
            sends[f].start()
    for copy in sends:
        copy.wait()


def side_kernel(
    counts_hbm, load_hbm, map_hbm, decay_hbm, out_hbm, area_ref, bus_ref, rule_ref, sens_hbm,
    knots_ref, levels_ref,
    flow_ref, table_ref,
    counts_ref, load_ref, map_ref, decay_ref, out_ref, sens_ref,
    load_sems, map_sems, sems,
):
    per_dev, span, scen, nodes = load_ref.shape
    lanes = flow_ref.shape[2]
    small = started(
        [
            (counts_hbm, counts_ref),
            (decay_hbm, decay_ref),
            (out_hbm, out_ref),
            (sens_hbm, sens_ref),
        ],
        sems,
    )
    loads, maps = started_feeders(load_hbm, load_ref, load_sems, map_hbm, map_ref, map_sems)
    areas = area_ref[...]
    rules = rule_ref[...]
    count = areas.shape[1]
    blocks = count // per_dev
    members = blocks * CAP
    slots, ranks = member_slots(areas, per_dev)
    me = lax.axis_index("feeder")
    feeder = lax.broadcasted_iota(jnp.int32, (per_dev, count), 1)
    here = feeder == me * per_dev + lax.broadcasted_iota(jnp.int32, (per_dev, count), 0)
    my_area = jnp.sum(jnp.where(here, areas, 0), axis=1, keepdims=True)
    my_rank = jnp.sum(jnp.where(here, ranks, 0), axis=1, keepdims=True)
    my_rule = jnp.sum(jnp.where(here, rules, 0), axis=1, keepdims=True)
    choice = lax.broadcasted_iota(jnp.int32, (per_dev, blocks), 1)
    hot = (choice == my_area).astype(F32)
    own = (areas == my_area).astype(F32)
    lane = lax.broadcasted_iota(jnp.int32, (per_dev, lanes), 1)
    of_rank = lax.div(lane, lanes // CAP) == my_rank
    of_k = lax.rem(lax.div(lane, members), 2)
    masks = [(of_rank & (of_k == k)).astype(F32) for k in range(2)]
    rule_count = knots_ref.shape[1]
    rule_choice = lax.broadcasted_iota(jnp.int32, (per_dev, rule_count), 1)
    rule_hot = (rule_choice == my_rule).astype(BF16)
    knots = knots_ref.shape[0]

    def looked_up(table_ref):
        high, low = split(table_ref[...].astype(F32))
        return (dot(rule_hot, high, NT) + dot(rule_hot, low, NT)) / 1000.0

    knot_volts = looked_up(knots_ref)
    knot_levels = looked_up(levels_ref)
    width = knot_volts[:, 1:] - knot_volts[:, : knots - 1]
    slope = (knot_levels[:, 1:] - knot_levels[:, : knots - 1]) / width
    table_ref[OWN, :, :] = own
    for k in range(2):
        table_ref[MASKS, :, k * lanes : (k + 1) * lanes] = masks[k]
    table_ref[HOT, :, :blocks] = hot
    table_ref[SLOT, :, :] = slots.astype(F32) + jnp.zeros((per_dev, count), F32)
    table_ref[KNOT, :, :knots] = knot_volts
    table_ref[KNOT, :, lanes : lanes + 1] = knot_levels[:, 0:1]
    table_ref[SLOPE, :, : knots - 1] = width
    table_ref[SLOPE, :, lanes : lanes + knots - 1] = slope
    for copy in small:
        copy.wait()
    planes = flow_ref.shape[0] - 1
    flow_ref[planes] = area_matrix(areas, slots, bus_ref[...], sens_ref, per_dev)
    state_id = lax.broadcasted_iota(jnp.int32, (1, map_ref.shape[2]), 1)
    for group in groups_of(GROUPS):
        for f in group:
            maps[f].wait()
            loads[f].wait()
        drives = drives_of(group, load_ref, map_ref)
        histories = [states_of(f, drive, decay_ref) for f, drive in zip(group, drives)]
        for f, history in zip(group, histories):
            out = jnp.where(state_id < counts_ref[f], out_ref[f], 0.0)
            flow = dot3(out, jnp.concatenate(history, 0), NT)
            for k in range(2):
                for piece in range(planes // 2):
                    flow_ref[k * (planes // 2) + piece, f : f + 1, :] = flow[
                        k : k + 1, piece * lanes : (piece + 1) * lanes
                    ]


def owner_kernel(recv_ref, out_ref, back_ref):
    chunks, rows, width = recv_ref.shape
    scen = back_ref.shape[2] // 2
    span = 6
    me = lax.axis_index("tm")
    out = out_ref[me]
    state = recv_ref[0, 0:scen]
    back_ref[0] = jnp.zeros(back_ref.shape[1:], F32)
    for chunk in range(1, chunks):
        product = recv_ref[chunk, scen : scen + 1]
        kept = [product]
        for t in range(1, span):
            product = product * recv_ref[chunk, scen + t : scen + t + 1]
            kept.append(product)
        blank = jnp.zeros((2, width), F32)
        even = [out[k : k + 1] * kept[t] for k in range(2) for t in range(0, span, 2)]
        odd = [out[k : k + 1] * kept[t] for k in range(2) for t in range(1, span, 2)]
        weights = jnp.concatenate(even + [blank] + odd + [blank], 0)
        flow = dot3(weights, state, NT)
        back_ref[chunk] = jnp.concatenate([flow[:8], flow[8:]], 1)[:span]
        if chunk < chunks - 1:
            state = recv_ref[chunk, 0:scen] + product * state


def join_kernel(back_ref, flow_ref, all_ref):
    planes = flow_ref.shape[0] - 1
    for plane in range(planes):
        all_ref[plane] = flow_ref[plane] + back_ref[:, plane, :]
    all_ref[planes] = flow_ref[planes]


def mix_kernel(knots, table_ref, every_ref, result_ref):
    blocks, planes, per_dev, lanes = every_ref.shape
    planes = planes - 1
    count = blocks * per_dev
    members = blocks * CAP
    me = lax.axis_index("feeder")
    hot = table_ref[HOT, :, :blocks].astype(BF16)
    masks = [
        table_ref[MASKS, :, k * lanes : (k + 1) * lanes].astype(BF16) for k in range(2)
    ]
    row = lax.rem(lax.broadcasted_iota(jnp.int32, (lanes, count), 0), members)
    spread = (row.astype(F32) == table_ref[SLOT, 0:1, :]).astype(BF16)
    high, low = split(every_ref[:, planes, pl.ds(me, 1), :].reshape(blocks, lanes))
    weight = jnp.zeros((2 * per_dev, count), F32)
    for part in (high, low):
        picked = dot(hot, part, NN).astype(BF16)
        weight = weight + dot(
            jnp.concatenate([picked * masks[0], picked * masks[1]], 0), spread, NN
        )
    own = table_ref[OWN]
    weights = [weight[k * per_dev : (k + 1) * per_dev] * own for k in range(2)]
    per_k = planes // 2
    scen = result_ref.shape[2]
    knot_volts = table_ref[KNOT, :, :knots]
    first = table_ref[KNOT, :, lanes : lanes + 1]
    widths = table_ref[SLOPE, :, : knots - 1]
    slopes = table_ref[SLOPE, :, lanes : lanes + knots - 1]
    for piece in range(per_k):
        volts = sum(
            dot3(weights[k], every_ref[:, k * per_k + piece].reshape(count, lanes), NN)
            for k in range(2)
        )
        result = first + jnp.zeros_like(volts)
        for j in range(knots - 1):
            result = result + slopes[:, j : j + 1] * jnp.minimum(
                jnp.maximum(volts - knot_volts[:, j : j + 1], 0.0), widths[:, j : j + 1]
            )
        result_ref[2 * piece] = result[:, :scen]
        result_ref[2 * piece + 1] = result[:, scen:]


def drive_call(counts, load, drive_map, decay):
    per_dev, span, scen, _ = load.shape
    width = drive_map.shape[2]
    rows = scen + span
    operands = (load, drive_map, decay)
    return pl.pallas_call(
        drive_kernel,
        in_specs=[ANYWHERE] * 4,
        out_specs=ANYWHERE,
        out_shape=jax.ShapeDtypeStruct((per_dev, rows, width), F32),
        scratch_shapes=[
            pltpu.VMEM((per_dev, rows, width), F32),
            pltpu.SMEM(counts.shape, counts.dtype),
        ]
        + [pltpu.VMEM(x.shape, x.dtype) for x in operands]
        + [pltpu.SemaphoreType.DMA((per_dev,))] * 3
        + [pltpu.SemaphoreType.DMA((2,))],
        compiler_params=pltpu.CompilerParams(vmem_limit_bytes=58 * 1024 * 1024),
        name="drive",
    )(counts, *operands)


def side_call(
    counts, load, drive_map, decay, out_map, area_row, bus_row, rule_row, sensitivity,
    knots, levels,
):
    per_dev, span, scen, nodes = load.shape
    width = drive_map.shape[2]
    lanes = 2 * scen
    count = area_row.shape[1]
    shapes = [(span + 1, per_dev, lanes), (6, per_dev, count)]
    copied = (load, drive_map, decay, out_map, sensitivity)
    return pl.pallas_call(
        side_kernel,
        in_specs=[ANYWHERE] * 5 + [WHOLE] * 3 + [ANYWHERE] + [WHOLE] * 2,
        out_specs=[WHOLE] * len(shapes),
        out_shape=[pltpu.VMEM(shape, F32) for shape in shapes],
        scratch_shapes=[pltpu.SMEM(counts.shape, counts.dtype)]
        + [pltpu.VMEM(x.shape, x.dtype) for x in copied]
        + [pltpu.SemaphoreType.DMA((per_dev,))] * 2
        + [pltpu.SemaphoreType.DMA((4,))],
        compiler_params=pltpu.CompilerParams(vmem_limit_bytes=56 * 1024 * 1024),
        cost_estimate=pl.CostEstimate(
            flops=2 * per_dev * span * scen * nodes * width,
            bytes_accessed=20 * 1024 * 1024,
            transcendentals=0,
        ),
        name="side",
    )(
        counts, load, drive_map, decay, out_map, area_row, bus_row, rule_row, sensitivity,
        knots, levels,
    )


def per_device(
    node_load, drive_map, decay_rate, counts, out_map, area_of, head_bus, rule_of,
    rule_knots, levels, sensitivity,
):
    per_dev, scen, span, nodes = node_load.shape
    feeders = area_of.shape[0]
    chunks = lax.axis_size("tm")
    lanes = 2 * scen
    load = jnp.transpose(node_load, (0, 2, 1, 3))
    decay = jnp.transpose(decay_rate, (1, 0, 2))

    send = drive_call(counts, load, drive_map, decay)
    owned = lax.all_to_all(send, "tm", 0, 0, tiled=True)
    flow, table = side_call(
        counts, load, drive_map, decay, out_map,
        jnp.transpose(area_of, (1, 0)), head_bus.reshape(1, feeders),
        rule_of.reshape(1, feeders), sensitivity,
        jnp.transpose(rule_knots, (1, 0)), jnp.transpose(levels, (1, 0)),
    )
    owned, flow, table = lax.optimization_barrier((owned, flow, table))
    back = pl.pallas_call(
        owner_kernel,
        in_specs=[WHOLE, WHOLE],
        out_specs=WHOLE,
        out_shape=pltpu.VMEM((chunks, span, lanes), F32),
        compiler_params=pltpu.CompilerParams(vmem_limit_bytes=16 * 1024 * 1024),
        name="owner",
    )(owned, out_map)
    back = lax.all_to_all(back, "tm", 0, 0, tiled=True)
    joined = pl.pallas_call(
        join_kernel,
        in_specs=[WHOLE] * 2,
        out_specs=WHOLE,
        out_shape=pltpu.VMEM(flow.shape, F32),
        compiler_params=pltpu.CompilerParams(vmem_limit_bytes=8 * 1024 * 1024),
        name="join",
    )(back, flow)
    every = lax.all_gather(joined, "feeder", axis=0, tiled=False)
    result = pl.pallas_call(
        functools.partial(mix_kernel, levels.shape[1]),
        in_specs=[WHOLE] * 2,
        out_specs=WHOLE,
        out_shape=jax.ShapeDtypeStruct((span, per_dev, scen), F32),
        compiler_params=pltpu.CompilerParams(vmem_limit_bytes=16 * 1024 * 1024),
        name="mix",
    )(table, every)
    return jnp.transpose(result, (1, 0, 2))


def solution(mesh):
    return jax.shard_map(
        per_device,
        mesh=mesh,
        in_specs=(
            P("feeder", None, "tm", None),
            P("feeder", None, None),
            P("feeder", "tm", None),
            P("feeder"),
            P("feeder", None, None),
            P(),
            P(),
            P(),
            P(),
            P(),
            P("feeder", None, None, None),
        ),
        out_specs=P("feeder", "tm", None),
        check_vma=False,
    )
```
